512 devices in a mesh: row: 16 (over y_lo, x), col: 8 (over z), scan: 4 (over y_hi, core).
Axes of the slice: x: 4, y: 8 (y_hi: 2, y_lo: 4; y = y_hi * 4 + y_lo), z: 8, core: 2. Of those that a mesh axis runs over, the one named last changes fastest.
Arguments:
- tokens: bfloat16 [64, 8, 2, 2, 128, 768], P(('scan', 'row'), 'col'), parts along dimension 0, may hold values from -6 to 6
- gain: float32 [768], replicated, may hold values from 0.5 to 1.5
- w_qkv: bfloat16 [768, 2304], replicated, may hold values from -2 to 2, as said below
- pattern: int32 [64, 8, 2, 2, 9], P(('scan', 'row'), 'col'), parts along dimension 0, may hold values 0 or 1
- counts: int32 [64, 8], P(('scan', 'row'), 'col'), parts along dimension 0, may hold values from 1 to 512, as said below
- region: int32 [1024], P('scan'), parts along dimension 0, may hold values from 0 to 65535, as said below
Outputs:
- attended: bfloat16 [64, 8, 2, 2, 128, 768], P(('scan', 'row'), 'col'), parts along dimension 0
The draws below stay inside these ranges and needn't reach their ends.
There are 4 independent parts, one for each index of `scan`. The reference program is written for one: setup_inputs(seed, part) draws one part's arguments, and reference() takes and returns one part's arrays. A program takes and returns all parts, laid end to end along the dimension named above; an argument that names none is the same for every part. Nothing has to cross between parts.
Inputs may be any that keep to these rules, and one draw needn't show every extreme that they name: `w_qkv`: the weights have entries of magnitude at most 2. `counts`: some tile has all 512 tokens valid. `region`: the indices are distinct.
All inputs are finite; a program needn't handle non-finite values. No bound on the sum of `pattern` on one device may be relied on, other than what follows from the above.
Results may differ from the reference program's by a relative error of at most 0.004.
The reference program's roundings to bfloat16 on the way count: a program that leaves them out, or rounds other values in their place, can miss the bound.
Values may be sent and summed in bfloat16 or wider, within the bound.
A program may use at most 64 MiB of HBM per device.

```python
import jax
import jax.numpy as jnp
from jax import lax

D = 768
HEADS = 12
HDIM = 64
BLK = 128
BR = 2
BC = 2
REGION = 256
TOKENS = 65536
N_ROW = 16
N_COL = 8


def draw_w_qkv(key, part):
    first = jax.random.fold_in(key, 0)
    scale = D ** (-0.5)
    whole = jnp.clip(jax.random.normal(first, (D, 3 * D), jnp.float32), -6.0, 6.0) * scale
    return jnp.clip(whole, -2.0, 2.0).astype(jnp.bfloat16)


def draw_counts(key, part):
    first, second, third = jax.random.split(key, 3)
    full = BR * BC * BLK
    whole_tile = jax.random.randint(first, (N_ROW * N_COL,), 0, 2)
    ragged = jax.random.randint(second, (N_ROW * N_COL,), 1, full + 1)
    counts = jnp.where(whole_tile == 1, full, ragged)
    chosen = jax.random.randint(third, (), 0, N_ROW * N_COL)
    counts = counts.at[chosen].set(full)
    return counts.reshape(N_ROW, N_COL).astype(jnp.int32)


def draw_region(key, part):
    first, second = jax.random.split(key, 2)
    inner = jax.random.permutation(first, TOKENS - 2)[:REGION - 2] + 1
    ends = jnp.array([0, TOKENS - 1], dtype=jnp.int32)
    picked = jnp.concatenate([ends, inner.astype(jnp.int32)])
    return jax.random.permutation(second, picked).astype(jnp.int32)


def touch_ends(entries, stream_key, smallest, top_value):
    longest = entries.shape.index(max(entries.shape))
    spots = []
    for shift in (0, 1):
        where = [jax.random.randint(jax.random.fold_in(stream_key, axis), (), 0, length) for axis, length in enumerate(entries.shape)]
        where[longest] = (where[longest] + shift) % entries.shape[longest]
        spots.append(tuple(where))
    return entries.at[spots[0]].set(smallest).at[spots[1]].set(top_value)


def shard_levels(stream_key, shape, cuts, low, largest):
    factor_of, own = 1.0, jax.random.fold_in(stream_key, 6)
    for dim, blocks in cuts:
        steps = jnp.exp(jax.random.uniform(jax.random.fold_in(own, dim), (blocks,), jnp.float32, low / len(cuts), largest / len(cuts)))
        factor_of = factor_of * jnp.repeat(steps, shape[dim] // blocks).reshape([-1 if axis == dim else 1 for axis in range(len(shape))])
    return factor_of


def gaussian(key, extent, width, reach, cuts=(), held_as=jnp.bfloat16):
    level = shard_levels(key, extent, cuts, -0.22, 0.18) if cuts else 1.0
    drawn = jax.random.normal(key, extent, jnp.float32) * width * level
    return jnp.minimum(jnp.maximum(drawn, -reach), reach).astype(held_as)


def setup_inputs(seed: int = 0, part: int = 0) -> dict:
    arg_keys = jax.random.split(jax.random.key(seed), 7)
    part_splits = jax.random.split(jax.random.fold_in(arg_keys[6], part), 7)
    return {
        "tokens": gaussian(part_splits[0], (N_ROW, N_COL, BR, BC, BLK, D), 1.0, 6.0, ((0, 16), (1, 8))),
        "gain": jnp.clip(1.0 + 0.1 * jax.random.normal(arg_keys[1], (D,), jnp.float32), 0.5, 1.5),
        "w_qkv": draw_w_qkv(jax.random.fold_in(arg_keys[6], 71), part),
        "pattern": touch_ends((jax.random.randint(part_splits[3], (N_ROW, N_COL, BR, BC, 9), 0, 2) < 1).astype(jnp.int32), jax.random.fold_in(part_splits[3], 1), 0, 1),
        "counts": draw_counts(jax.random.fold_in(jax.random.fold_in(arg_keys[6], part), 71), part),
        "region": draw_region(jax.random.fold_in(jax.random.fold_in(arg_keys[6], part), 71), part),
    }


def layer_norm(values, gain):
    floats = values.astype(jnp.float32)
    center = floats - lax.optimization_barrier(jnp.mean(floats, axis=-1, keepdims=True))
    spread = lax.optimization_barrier(jnp.mean(center * center, axis=-1, keepdims=True))
    return (center * lax.rsqrt(spread + 1e-05) * gain).astype(jnp.bfloat16)

def to_grid(array):
    order = (0, 2, 1, 3) + tuple(range(4, array.ndim))
    moved = jnp.transpose(array, order)
    return moved.reshape((N_ROW * BR, N_COL * BC) + array.shape[4:])

def reference(tokens, gain, w_qkv, pattern, counts, region):
    normed = layer_norm(tokens, gain)
    tiles = normed.reshape(N_ROW * N_COL, BR * BC * BLK, D)
    qkv = lax.map(lambda rows: jnp.dot(rows, w_qkv, preferred_element_type=jnp.float32).astype(jnp.bfloat16), tiles)
    flat = qkv.reshape(-1, 3 * D)
    region_k = jnp.take(flat[:, D:2 * D], region, axis=0)
    region_v = jnp.take(flat[:, 2 * D:], region, axis=0)
    shaped = qkv.reshape(N_ROW, N_COL, BR, BC, BLK, 3 * D)
    query = to_grid(shaped[..., :D])
    keys = jnp.pad(to_grid(shaped[..., D:2 * D]), ((1, 1), (1, 1), (0, 0), (0, 0)))
    values = jnp.pad(to_grid(shaped[..., 2 * D:]), ((1, 1), (1, 1), (0, 0), (0, 0)))
    position = jnp.arange(BR * BC * BLK, dtype=jnp.int32).reshape(BR, BC, BLK)
    valid = position[None, None] < counts[:, :, None, None, None]
    valid_grid = to_grid(valid)
    valid_pad = jnp.pad(valid_grid, ((1, 1), (1, 1), (0, 0)))
    pattern_grid = to_grid(pattern) > 0
    columns = N_COL * BC
    scale = HDIM ** (-0.5)

    def one_row(index):
        q_row = query[index].astype(jnp.float32).reshape(columns, BLK, HEADS, HDIM)
        key_list = []
        value_list = []
        mask_list = []
        for drow in range(3):
            k_line = lax.dynamic_index_in_dim(keys, index + drow, 0, keepdims=False)
            v_line = lax.dynamic_index_in_dim(values, index + drow, 0, keepdims=False)
            m_line = lax.dynamic_index_in_dim(valid_pad, index + drow, 0, keepdims=False)
            for dcol in range(3):
                key_list.append(k_line[dcol:dcol + columns])
                value_list.append(v_line[dcol:dcol + columns])
                allowed = lax.dynamic_index_in_dim(pattern_grid, index, 0, keepdims=False)[:, 3 * drow + dcol]
                mask_list.append(m_line[dcol:dcol + columns] & allowed[:, None])
        near_k = jnp.concatenate(key_list, axis=1)
        near_v = jnp.concatenate(value_list, axis=1)
        near_m = jnp.concatenate(mask_list, axis=1)
        all_k = jnp.concatenate([near_k, jnp.broadcast_to(region_k[None], (columns, REGION, D))], axis=1)
        all_v = jnp.concatenate([near_v, jnp.broadcast_to(region_v[None], (columns, REGION, D))], axis=1)
        all_m = jnp.concatenate([near_m, jnp.ones((columns, REGION), bool)], axis=1)
        k_heads = all_k.astype(jnp.float32).reshape(columns, -1, HEADS, HDIM)
        v_heads = all_v.astype(jnp.float32).reshape(columns, -1, HEADS, HDIM)
        scores = jnp.einsum('cqhd,ckhd->chqk', q_row, k_heads) * scale
        mask = all_m[:, None, None, :]
        masked = jnp.where(mask, scores, -1e+30)
        top = lax.optimization_barrier(jnp.max(masked, axis=-1, keepdims=True))
        weights = jnp.where(mask, jnp.exp(masked - top), 0.0)
        total = lax.optimization_barrier(jnp.sum(weights, axis=-1, keepdims=True))
        probs = (weights / total).astype(jnp.bfloat16)
        out = jnp.einsum('chqk,ckhd->cqhd', probs.astype(jnp.float32), v_heads).astype(jnp.bfloat16)
        out = out.reshape(columns, BLK, D)
        live = lax.dynamic_index_in_dim(valid_grid, index, 0, keepdims=False)
        return jnp.where(live[:, :, None], out, jnp.zeros_like(out))
    result = lax.map(one_row, jnp.arange(N_ROW * BR, dtype=jnp.int32))
    result = result.reshape(N_ROW, BR, N_COL, BC, BLK, D)
    return jnp.transpose(result, (0, 2, 1, 3, 4, 5))
```

```python
import functools

import jax
import jax.numpy as jnp
from jax import lax
from jax.experimental import pallas as pl
from jax.experimental.pallas import tpu as pltpu
from jax.sharding import PartitionSpec as P

HEADS = 12
HDIM = 64
BLK = 128
WIDTH = HEADS * HDIM
AUG = 2 * HDIM
REGION = 256
MESH = pl.DeviceIdType.MESH
EXP_SCALE = (HDIM ** (-0.5)) * 1.4426950408889634
FAR = -1e30
LOW, HIGH = 2.0 ** (-80), 2.0**100

SLOTS = ((0, 1), (0, 2), (3, 1), (3, 2), (1, 0), (2, 0), (1, 3), (2, 3), (0, 0), (0, 3), (3, 0), (3, 3))
OWN = ((1, 1), (1, 2), (2, 1), (2, 2))
OWN_KEYS = 4 * BLK
HALO_KEYS = len(SLOTS) * BLK
REGION_AT = OWN_KEYS + HALO_KEYS
KEYS = REGION_AT + REGION


def dot(a, b):
    return lax.dot_general(a, b, (((1,), (0,)), ((), ())), preferred_element_type=jnp.float32)


def dot_t(a, b):
    return lax.dot_general(a, b, (((1,), (1,)), ((), ())), preferred_element_type=jnp.float32)


def norm_rows(values, gain):
    floats = values.astype(jnp.float32)
    center = floats - jnp.sum(floats, axis=-1, keepdims=True) * (1.0 / WIDTH)
    spread = jnp.sum(center * center, axis=-1, keepdims=True) * (1.0 / WIDTH)
    return (center * lax.rsqrt(spread + 1e-05) * gain).astype(jnp.bfloat16)


def tile_of(place):
    return tuple((0, 1, 1, 2)[p] for p in place), tuple((1, 0, 1, 0)[p] for p in place)


def kernel(
    n_row, n_col,
    tok_hbm, gain_ref, w_hbm, pat_ref, cnt_ref, reg_ref,
    out_ref, flag_ref, halo_out, rtok_out, cnts_out,
    own, halo, weights, cnts, picks, part1, mine, part2, rtok, normed, qa, ka, va, oa,
    load_sem, halo_send, halo_recv, cnt_send, cnt_recv, p1_send, p1_recv, p2_send, p2_recv, p3_send, p3_recv, save_sem,
):
    row, col = lax.axis_index("row"), lax.axis_index("col")
    up, down, left, right = row > 0, row < n_row - 1, col > 0, col < n_col - 1
    exists_r, exists_c = (up, None, None, down), (left, None, None, right)
    chunk = REGION // n_row

    def both(a, b):
        return b if a is None else (a if b is None else a & b)

    def there(place):
        return both(exists_r[place[0]], exists_c[place[1]])

    loads = [
        pltpu.make_async_copy(tok_hbm, own, load_sem.at[0]),
        pltpu.make_async_copy(w_hbm, weights, load_sem.at[1]),
    ]
    for load in loads:
        load.start()

    barrier = pltpu.get_barrier_semaphore()
    diagonals = [(dr, dc) for dr in (-1, 1) for dc in (-1, 1)]

    def signal_row(r, _):
        @pl.when(r != row)
        def _():
            pl.semaphore_signal(barrier, inc=1, device_id={"row": r}, device_id_type=MESH)
        return 0

    def signal_col(c, _):
        @pl.when(c != col)
        def _():
            pl.semaphore_signal(barrier, inc=1, device_id={"col": c}, device_id_type=MESH)
        return 0

    lax.fori_loop(0, n_row, signal_row, 0)
    lax.fori_loop(0, n_col, signal_col, 0)
    for dr, dc in diagonals:
        @pl.when(both(up if dr < 0 else down, left if dc < 0 else right))
        def _(dr=dr, dc=dc):
            pl.semaphore_signal(barrier, inc=1, device_id={"row": row + dr, "col": col + dc}, device_id_type=MESH)

    as_int = lambda flag: jnp.where(flag, 1, 0)
    n_diag = (as_int(up) + as_int(down)) * (as_int(left) + as_int(right))

    for group in range(4):
        @pl.when(jnp.logical_not((up, down, left, right)[group]))
        def _(group=group):
            halo[2 * group : 2 * group + 2] = jnp.zeros((2, BLK, WIDTH), jnp.bfloat16)
    for slot in range(8, 12):
        @pl.when(jnp.logical_not(there(SLOTS[slot])))
        def _(slot=slot):
            halo[slot] = jnp.zeros((BLK, WIDTH), jnp.bfloat16)
    count = cnt_ref[0, 0]
    for t in range(9):
        if t == 4:
            cnts[t] = jnp.broadcast_to(count, (8, 128)).astype(jnp.int32)
        else:
            dr, dc = t // 3 - 1, t % 3 - 1
            exists = both((up, None, down)[dr + 1], (left, None, right)[dc + 1])

            @pl.when(jnp.logical_not(exists))
            def _(t=t):
                cnts[t] = jnp.zeros((8, 128), jnp.int32)

    loads[0].wait()
    pl.semaphore_wait(barrier, n_row + n_col - 2 + n_diag)

    def remote(src, dst, send, recv, device):
        return pltpu.make_async_remote_copy(
            src_ref=src, dst_ref=dst, send_sem=send, recv_sem=recv, device_id=device, device_id_type=MESH
        )

    sends = []

    def send_halo(cond, src, slot, device):
        copy = remote(src, halo.at[slot], halo_send.at[len(sends)], halo_recv.at[slot], device)
        sends.append((cond, copy))
        pl.when(cond)(lambda: copy.start())

    def halo_wait(slots):
        for slot in slots:
            copy = remote(halo.at[slot], halo.at[slot], halo_send.at[slot], halo_recv.at[slot], {"row": row})
            pl.when(there(SLOTS[slot]))(lambda copy=copy: copy.wait_recv())

    send_halo(up, own.at[0], 2, {"row": row - 1})
    send_halo(up, own.at[1], 3, {"row": row - 1})
    send_halo(down, own.at[2], 0, {"row": row + 1})
    send_halo(down, own.at[3], 1, {"row": row + 1})

    cnt_copies = []
    for t in range(9):
        if t != 4:
            dr, dc = t // 3 - 1, t % 3 - 1
            exists = both((up, None, down)[dr + 1], (left, None, right)[dc + 1])
            device = {}
            if dr:
                device["row"] = row + dr
            if dc:
                device["col"] = col + dc
            copy = remote(cnts.at[4], cnts.at[8 - t], cnt_send.at[t], cnt_recv.at[8 - t], device)
            arrives = remote(cnts.at[4], cnts.at[t], cnt_send.at[t], cnt_recv.at[t], device)
            cnt_copies.append((exists, copy, arrives))
            pl.when(exists)(lambda copy=copy: copy.start())

    tokens = own[...].reshape(OWN_KEYS, WIDTH)
    first = (row * n_col + col) * OWN_KEYS
    flat = lax.broadcasted_iota(jnp.int32, (OWN_KEYS, REGION), 0) + first
    hit = jnp.where(flat == reg_ref[...], 1.0, 0.0).astype(jnp.bfloat16)
    found = lax.dot_general(hit, tokens, (((0,), (0,)), ((), ())), preferred_element_type=jnp.float32)
    picks[...] = found.astype(jnp.bfloat16).reshape(n_row, chunk, WIDTH)

    def exchange(size, axis, me, source, target, send_sem, recv_sem):
        def copy_to(k):
            return remote(source(k), target(me), send_sem.at[k], recv_sem.at[me], {axis: k})

        def copy_from(k):
            return remote(source(k), target(k), send_sem.at[k], recv_sem.at[k], {axis: k})

        def start(k, _):
            pl.when(k != me)(lambda: copy_to(k).start())
            return 0

        def arrive(k, _):
            pl.when(k != me)(lambda: copy_from(k).wait_recv())
            return 0

        def leave(k, _):
            pl.when(k != me)(lambda: copy_to(k).wait_send())
            return 0

        return tuple(lambda body=body: lax.fori_loop(0, size, body, 0) for body in (start, arrive, leave))

    start1, arrive1, leave1 = exchange(
        n_row, "row", row, lambda k: picks.at[k], lambda k: part1.at[k], p1_send, p1_recv
    )
    start2, arrive2, leave2 = exchange(n_col, "col", col, lambda k: mine, lambda k: part2.at[k], p2_send, p2_recv)
    start3, arrive3, leave3 = exchange(
        n_row, "row", row, lambda k: rtok.at[row], lambda k: rtok.at[k], p3_send, p3_recv
    )
    start1()
    part1[row] = picks[row]

    send_halo(left, own.at[0], 6, {"col": col - 1})
    send_halo(left, own.at[2], 7, {"col": col - 1})
    send_halo(right, own.at[1], 4, {"col": col + 1})
    send_halo(right, own.at[3], 5, {"col": col + 1})

    lane = lax.broadcasted_iota(jnp.int32, (1, AUG), 1)
    spare = lax.rem(lane, HDIM)
    low_half = lane < HDIM

    def query_marks(block):
        i, j = divmod(block, 2)
        marks = jnp.where(spare == 16, FAR, 0.0)
        for k in range(9):
            place = (i + k // 3, j + k % 3)
            allowed = pat_ref[block, k].astype(jnp.float32)
            exists = there(place)
            if exists is not None:
                allowed = allowed * as_int(exists).astype(jnp.float32)
            marks = jnp.where(spare == place[0] * 4 + place[1], (1.0 - allowed) * FAR, marks)
        return marks

    def key_marks(place):
        (tr, tc), (i, j) = tile_of(place)
        position = lax.broadcasted_iota(jnp.int32, (BLK, AUG), 0) + (i * 2 + j) * BLK
        beyond = jnp.where(position >= cnts[3 * tr + tc, 0:1, :], 1.0, 0.0)
        return jnp.where(spare == 16, beyond, jnp.where(spare == place[0] * 4 + place[1], 1.0, 0.0))

    def halves(pair, other):
        return jnp.where(low_half, pair, other), jnp.where(low_half, other, pair)

    def project(rows, key_at, marks, part, out):
        n = rows

        def body(j, _):
            at = pl.multiple_of(part * WIDTH + j * 256, 128)
            result = dot(normed[0:n, :], weights[:, pl.ds(at, 256)]).astype(jnp.bfloat16)
            for t in range(2):
                pair = result[:, t * 128 : t * 128 + 128]
                first_head, second_head = halves(pair, marks)
                to = pl.multiple_of(j * 512 + t * 256, 128)
                out[pl.ds(key_at, n), pl.ds(to, 128)] = first_head
                out[pl.ds(key_at, n), pl.ds(pl.multiple_of(to + 128, 128), 128)] = second_head
            return 0

        lax.fori_loop(0, 3, body, 0)

    def keys_values(values, key_at, places):
        n = values.shape[0]
        normed[0:n, :] = norm_rows(values, gain_ref[...])
        if places is None:
            marks = jnp.zeros((n, AUG), jnp.bfloat16)
        else:
            marks = jnp.concatenate([key_marks(place) for place in places], axis=0).astype(jnp.bfloat16)
        project(n, key_at, marks, 1, ka)
        project(n, key_at, jnp.ones((n, AUG), jnp.bfloat16), 2, va)

    def attend(blocks, key_at, n, initial=False):
        def body(h, _):
            at = pl.ds(pl.multiple_of(h * AUG, 128), AUG)
            if len(blocks) == 4:
                q = qa[:, at]
            else:
                q = jnp.concatenate([qa[pl.ds(b * BLK, BLK), at] for b in blocks], axis=0)
            scores = dot_t(q, ka[pl.ds(key_at, n), at])
            probs = jnp.exp2(scores * EXP_SCALE).astype(jnp.bfloat16)
            result = dot(probs, va[pl.ds(key_at, n), at])
            if initial:
                oa[:, at] = result
            else:
                for s, b in enumerate(blocks):
                    oa[pl.ds(b * BLK, BLK), at] += result[s * BLK : s * BLK + BLK]
            return 0

        lax.fori_loop(0, HEADS, body, 0)

    loads[1].wait()
    keys_values(tokens, 0, OWN)
    q_marks = jnp.concatenate([jnp.broadcast_to(query_marks(b), (BLK, AUG)) for b in range(4)], axis=0)
    project(OWN_KEYS, 0, q_marks.astype(jnp.bfloat16), 0, qa)

    arrive1()
    total = part1[0].astype(jnp.float32)
    for k in range(1, n_row):
        total = total + part1[k].astype(jnp.float32)
    mine[...] = total.astype(jnp.bfloat16)
    start2()
    part2[col] = mine[...]

    halo_wait((0, 1, 2, 3))
    send_halo(both(up, left), halo.at[0], 9, {"col": col - 1})
    send_halo(both(up, right), halo.at[1], 8, {"col": col + 1})
    send_halo(both(down, left), halo.at[2], 11, {"col": col - 1})
    send_halo(both(down, right), halo.at[3], 10, {"col": col + 1})

    attend((0, 1, 2, 3), 0, OWN_KEYS, initial=True)

    arrive2()
    total = part2[0].astype(jnp.float32)
    for k in range(1, n_col):
        total = total + part2[k].astype(jnp.float32)
    rtok[row] = total.astype(jnp.bfloat16)
    start3()

    for exists, _, arrives in cnt_copies:
        pl.when(exists)(lambda arrives=arrives: arrives.wait_recv())

    for group, blocks in enumerate(((0, 1), (2, 3), (0, 2), (1, 3))):
        slots = (2 * group, 2 * group + 1)
        if group >= 2:
            halo_wait(slots)
        key_at = OWN_KEYS + 2 * group * BLK
        keys_values(halo[2 * group : 2 * group + 2].reshape(2 * BLK, WIDTH), key_at, [SLOTS[s] for s in slots])
        attend(blocks, key_at, 2 * BLK)

    arrive3()
    keys_values(rtok[...].reshape(REGION, WIDTH), REGION_AT, None)
    attend((0, 1, 2, 3), REGION_AT, REGION)

    halo_wait((8, 9, 10, 11))
    saves = [
        pltpu.make_async_copy(halo, halo_out, save_sem.at[0]),
        pltpu.make_async_copy(rtok, rtok_out, save_sem.at[1]),
        pltpu.make_async_copy(cnts, cnts_out, save_sem.at[2]),
    ]
    for save in saves:
        save.start()
    keys_values(halo[8:12].reshape(4 * BLK, WIDTH), OWN_KEYS + 8 * BLK, SLOTS[8:12])
    for b in range(4):
        attend((b,), OWN_KEYS + (8 + b) * BLK, BLK)

    valid = lax.broadcasted_iota(jnp.int32, (OWN_KEYS, AUG), 0) < count

    def finish(p, bad):
        one = oa[:, pl.ds(pl.multiple_of(p * 256, 128), 128)]
        two = oa[:, pl.ds(pl.multiple_of(p * 256 + 128, 128), 128)]
        sums = pltpu.roll(jnp.where(low_half, two, one), HDIM, 1)
        result = jnp.where(low_half, one, two) / sums
        out_ref[:, pl.ds(pl.multiple_of(p * 128, 128), 128)] = jnp.where(valid, result, 0.0).astype(jnp.bfloat16)
        fine = (sums >= LOW) & (sums <= HIGH)
        return jnp.maximum(bad, jnp.max(jnp.where(fine, 0.0, 1.0), axis=0, keepdims=True))

    bad = lax.fori_loop(0, 6, finish, jnp.zeros((1, AUG), jnp.float32))
    flag_ref[...] = jnp.broadcast_to(bad, (8, AUG))

    for cond, copy in sends:
        pl.when(cond)(lambda copy=copy: copy.wait_send())
    for exists, copy, _ in cnt_copies:
        pl.when(exists)(lambda copy=copy: copy.wait_send())
    leave1()
    leave2()
    leave3()
    for save in saves:
        save.wait()


def fused(n_row, n_col, tokens, gain, w_qkv, pattern, counts, region):
    chunk = REGION // n_row
    vmem = pl.BlockSpec(memory_space=pltpu.VMEM)
    smem = pl.BlockSpec(memory_space=pltpu.SMEM)
    anywhere = pl.BlockSpec(memory_space=pl.ANY)
    bf16, f32 = jnp.bfloat16, jnp.float32
    dma = pltpu.SemaphoreType.DMA
    flops = 2 * (OWN_KEYS * WIDTH * WIDTH * 3 + (KEYS - OWN_KEYS) * WIDTH * WIDTH * 2 + OWN_KEYS * 1408 * WIDTH * 2)
    return pl.pallas_call(
        functools.partial(kernel, n_row, n_col),
        out_shape=(
            jax.ShapeDtypeStruct((OWN_KEYS, WIDTH), bf16),
            jax.ShapeDtypeStruct((8, AUG), f32),
            jax.ShapeDtypeStruct((len(SLOTS), BLK, WIDTH), bf16),
            jax.ShapeDtypeStruct((n_row, chunk, WIDTH), bf16),
            jax.ShapeDtypeStruct((9, 8, 128), jnp.int32),
        ),
        in_specs=[anywhere, vmem, anywhere, smem, smem, vmem],
        out_specs=(vmem, vmem, anywhere, anywhere, anywhere),
        scratch_shapes=[
            pltpu.VMEM((4, BLK, WIDTH), bf16),
            pltpu.VMEM((len(SLOTS), BLK, WIDTH), bf16),
            pltpu.VMEM((WIDTH, 3 * WIDTH), bf16),
            pltpu.VMEM((9, 8, 128), jnp.int32),
            pltpu.VMEM((n_row, chunk, WIDTH), bf16),
            pltpu.VMEM((n_row, chunk, WIDTH), bf16),
            pltpu.VMEM((chunk, WIDTH), bf16),
            pltpu.VMEM((n_col, chunk, WIDTH), bf16),
            pltpu.VMEM((n_row, chunk, WIDTH), bf16),
            pltpu.VMEM((OWN_KEYS, WIDTH), bf16),
            pltpu.VMEM((OWN_KEYS, HEADS * AUG), bf16),
            pltpu.VMEM((KEYS, HEADS * AUG), bf16),
            pltpu.VMEM((KEYS, HEADS * AUG), bf16),
            pltpu.VMEM((OWN_KEYS, HEADS * AUG), f32),
            dma((2,)),
            dma((12,)), dma((12,)),
            dma((9,)), dma((9,)),
            dma((n_row,)), dma((n_row,)),
            dma((n_col,)), dma((n_col,)),
            dma((n_row,)), dma((n_row,)),
            dma((3,)),
        ],
        compiler_params=pltpu.CompilerParams(
            collective_id=0, has_side_effects=True, vmem_limit_bytes=48 << 20
        ),
        cost_estimate=pl.CostEstimate(flops=flops, bytes_accessed=9 << 20, transcendentals=OWN_KEYS * 1408 * HEADS),
    )(tokens, gain, w_qkv, pattern, counts, region)


def stable(own, gain, w_qkv, pattern, row, col, n_row, n_col, halo, rtok, cnts):
    grid = {place: own[i] for i, place in enumerate(OWN)}
    grid.update({place: halo[i] for i, place in enumerate(SLOTS)})
    places = [(r, c) for r in range(4) for c in range(4)]
    rows = jnp.concatenate([grid[p] for p in places] + [rtok.reshape(REGION, WIDTH)], axis=0)
    qkv = dot(norm_rows(rows, gain), w_qkv).astype(jnp.bfloat16)
    valid = []
    for place in places:
        (tr, tc), (i, j) = tile_of(place)
        valid.append(jnp.arange(BLK) + (i * 2 + j) * BLK < cnts[3 * tr + tc, 0, 0])
    masks = []
    for block in range(4):
        i, j = divmod(block, 2)
        marks = []
        for number, (r, c) in enumerate(places):
            dr, dc = r - i, c - j
            if 0 <= dr < 3 and 0 <= dc < 3:
                a, b = row * 2 + r - 1, col * 2 + c - 1
                inside = (a >= 0) & (a < 2 * n_row) & (b >= 0) & (b < 2 * n_col)
                marks.append(valid[number] & inside & (pattern[block, 3 * dr + dc] > 0))
            else:
                marks.append(jnp.zeros((BLK,), bool))
        masks.append(jnp.concatenate(marks + [jnp.ones((REGION,), bool)]))
    mask = jnp.stack(masks)
    own_at = jnp.array([4 * r + c for r, c in OWN])
    query = qkv[: 16 * BLK, :WIDTH].reshape(16, BLK, HEADS, HDIM)[own_at]
    key = qkv[:, WIDTH : 2 * WIDTH].reshape(-1, HEADS, HDIM)
    value = qkv[:, 2 * WIDTH :].reshape(-1, HEADS, HDIM)

    def one_head(args):
        q, k, v = args
        scores = jnp.einsum("bqd,kd->bqk", q, k, preferred_element_type=jnp.float32) * (HDIM ** (-0.5))
        masked = jnp.where(mask[:, None, :], scores, -1e30)
        top = jnp.max(masked, axis=-1, keepdims=True)
        weights = jnp.where(mask[:, None, :], jnp.exp(masked - top), 0.0)
        probs = (weights / jnp.sum(weights, axis=-1, keepdims=True)).astype(jnp.bfloat16)
        return jnp.einsum("bqk,kd->bqd", probs, v, preferred_element_type=jnp.float32).astype(jnp.bfloat16)

    heads = lax.map(one_head, (query.transpose(2, 0, 1, 3), key.transpose(1, 0, 2), value.transpose(1, 0, 2)))
    joined = heads.transpose(1, 2, 0, 3).reshape(OWN_KEYS, WIDTH)
    live = jnp.arange(OWN_KEYS) < cnts[4, 0, 0]
    return jnp.where(live[:, None], joined, jnp.zeros_like(joined))


def local(n_row, n_col, tokens, gain, w_qkv, pattern, counts, region):
    own = tokens.reshape(4, BLK, WIDTH)
    blocks = pattern.reshape(4, 9)
    scale = gain.reshape(1, WIDTH)
    out, flag, halo, rtok, cnts = fused(
        n_row, n_col, own, scale, w_qkv, blocks, counts, region.reshape(1, REGION)
    )
    row, col = lax.axis_index("row"), lax.axis_index("col")
    result = lax.cond(
        jnp.max(flag) > 0.0,
        lambda: stable(own, scale, w_qkv, blocks, row, col, n_row, n_col, halo, rtok, cnts),
        lambda: out,
    )
    return result.reshape(tokens.shape)


def solution(mesh):
    in_specs = (
        P(("scan", "row"), "col", None, None, None, None),
        P(),
        P(),
        P(("scan", "row"), "col", None, None, None),
        P(("scan", "row"), "col"),
        P("scan"),
    )
    out_specs = P(("scan", "row"), "col", None, None, None, None)
    body = functools.partial(local, mesh.shape["row"], mesh.shape["col"])
    return jax.shard_map(body, mesh=mesh, in_specs=in_specs, out_specs=out_specs, check_vma=False)
```

```python
import functools

import jax
import jax.numpy as jnp
from jax import lax
from jax.experimental import pallas as pl
from jax.experimental.layout import Layout, with_layout_constraint
from jax.experimental.pallas import tpu as pltpu
from jax.sharding import PartitionSpec as P

HEADS = 12
HDIM = 64
BLK = 128
WIDTH = HEADS * HDIM
AUG = 2 * HDIM
REGION = 256
MESH = pl.DeviceIdType.MESH
EXP_SCALE = (HDIM ** (-0.5)) * 1.4426950408889634
FAR = -1e30
LOW, HIGH = 2.0 ** (-80), 2.0**100

SLOTS = ((0, 1), (0, 2), (3, 1), (3, 2), (1, 0), (2, 0), (1, 3), (2, 3), (0, 0), (0, 3), (3, 0), (3, 3))
OWN = ((1, 1), (1, 2), (2, 1), (2, 2))
OWN_KEYS = 4 * BLK
HALO_KEYS = len(SLOTS) * BLK
REGION_AT = OWN_KEYS + HALO_KEYS
KEYS = REGION_AT + REGION


def dot(a, b):
    return lax.dot_general(a, b, (((1,), (0,)), ((), ())), preferred_element_type=jnp.float32)


def dot_t(a, b):
    return lax.dot_general(a, b, (((1,), (1,)), ((), ())), preferred_element_type=jnp.float32)


def norm_rows(values, gain):
    floats = values.astype(jnp.float32)
    center = floats - jnp.sum(floats, axis=-1, keepdims=True) * (1.0 / WIDTH)
    spread = jnp.sum(center * center, axis=-1, keepdims=True) * (1.0 / WIDTH)
    return (center * lax.rsqrt(spread + 1e-05) * gain).astype(jnp.bfloat16)


def tile_of(place):
    return tuple((0, 1, 1, 2)[p] for p in place), tuple((1, 0, 1, 0)[p] for p in place)


def kernel(
    n_row, n_col,
    tok_hbm, gain_ref, w_hbm, pat_ref, cnt_ref, reg_ref,
    out_ref, flag_ref, halo_out, rtok_out, cnts_out,
    own, halo, weights, cnts, picks, part1, mine, part2, rtok, normed, qa, ka, va, oa,
    load_sem, halo_send, halo_recv, cnt_send, cnt_recv, p1_send, p1_recv, p2_send, p2_recv, p3_send, p3_recv, save_sem,
):
    row, col = lax.axis_index("row"), lax.axis_index("col")
    up, down, left, right = row > 0, row < n_row - 1, col > 0, col < n_col - 1
    exists_r, exists_c = (up, None, None, down), (left, None, None, right)
    chunk = REGION // n_row

    def both(a, b):
        return b if a is None else (a if b is None else a & b)

    def there(place):
        return both(exists_r[place[0]], exists_c[place[1]])

    loads = [
        pltpu.make_async_copy(tok_hbm, own, load_sem.at[0]),
        pltpu.make_async_copy(w_hbm, weights, load_sem.at[1]),
    ]
    for load in loads:
        load.start()

    barrier = pltpu.get_barrier_semaphore()
    diagonals = [(dr, dc) for dr in (-1, 1) for dc in (-1, 1)]

    def signal_row(r, _):
        @pl.when(r != row)
        def _():
            pl.semaphore_signal(barrier, inc=1, device_id={"row": r}, device_id_type=MESH)
        return 0

    def signal_col(c, _):
        @pl.when(c != col)
        def _():
            pl.semaphore_signal(barrier, inc=1, device_id={"col": c}, device_id_type=MESH)
        return 0

    lax.fori_loop(0, n_row, signal_row, 0)
    lax.fori_loop(0, n_col, signal_col, 0)
    for dr, dc in diagonals:
        @pl.when(both(up if dr < 0 else down, left if dc < 0 else right))
        def _(dr=dr, dc=dc):
            pl.semaphore_signal(barrier, inc=1, device_id={"row": row + dr, "col": col + dc}, device_id_type=MESH)

    as_int = lambda flag: jnp.where(flag, 1, 0)
    n_diag = (as_int(up) + as_int(down)) * (as_int(left) + as_int(right))

    for group in range(4):
        @pl.when(jnp.logical_not((up, down, left, right)[group]))
        def _(group=group):
            halo[2 * group : 2 * group + 2] = jnp.zeros((2, BLK, WIDTH), jnp.bfloat16)
    for slot in range(8, 12):
        @pl.when(jnp.logical_not(there(SLOTS[slot])))
        def _(slot=slot):
            halo[slot] = jnp.zeros((BLK, WIDTH), jnp.bfloat16)
    count = cnt_ref[0, 0]
    for t in range(9):
        if t == 4:
            cnts[t] = jnp.broadcast_to(count, (8, 128)).astype(jnp.int32)
        else:
            dr, dc = t // 3 - 1, t % 3 - 1
            exists = both((up, None, down)[dr + 1], (left, None, right)[dc + 1])

            @pl.when(jnp.logical_not(exists))
            def _(t=t):
                cnts[t] = jnp.zeros((8, 128), jnp.int32)

    loads[0].wait()
    pl.semaphore_wait(barrier, n_row + n_col - 2 + n_diag)

    def remote(src, dst, send, recv, device):
        return pltpu.make_async_remote_copy(
            src_ref=src, dst_ref=dst, send_sem=send, recv_sem=recv, device_id=device, device_id_type=MESH
        )

    sends = []

    def send_halo(cond, src, slot, device):
        copy = remote(src, halo.at[slot], halo_send.at[len(sends)], halo_recv.at[slot], device)
        sends.append((cond, copy))
        pl.when(cond)(lambda: copy.start())

    def halo_wait(slots):
        for slot in slots:
            copy = remote(halo.at[slot], halo.at[slot], halo_send.at[slot], halo_recv.at[slot], {"row": row})
            pl.when(there(SLOTS[slot]))(lambda copy=copy: copy.wait_recv())

    send_halo(up, own.at[0], 2, {"row": row - 1})
    send_halo(up, own.at[1], 3, {"row": row - 1})
    send_halo(down, own.at[2], 0, {"row": row + 1})
    send_halo(down, own.at[3], 1, {"row": row + 1})

    cnt_copies = []
    for t in range(9):
        if t != 4:
            dr, dc = t // 3 - 1, t % 3 - 1
            exists = both((up, None, down)[dr + 1], (left, None, right)[dc + 1])
            device = {}
            if dr:
                device["row"] = row + dr
            if dc:
                device["col"] = col + dc
            copy = remote(cnts.at[4], cnts.at[8 - t], cnt_send.at[t], cnt_recv.at[8 - t], device)
            arrives = remote(cnts.at[4], cnts.at[t], cnt_send.at[t], cnt_recv.at[t], device)
            cnt_copies.append((exists, copy, arrives))
            pl.when(exists)(lambda copy=copy: copy.start())

    tokens = own[...].reshape(OWN_KEYS, WIDTH)
    first = (row * n_col + col) * OWN_KEYS
    flat = lax.broadcasted_iota(jnp.int32, (OWN_KEYS, REGION), 0) + first
    hit = jnp.where(flat == reg_ref[...], 1.0, 0.0).astype(jnp.bfloat16)
    found = lax.dot_general(hit, tokens, (((0,), (0,)), ((), ())), preferred_element_type=jnp.float32)
    picks[...] = found.astype(jnp.bfloat16).reshape(n_row, chunk, WIDTH)

    def exchange(size, axis, me, source, target, send_sem, recv_sem):
        def copy_to(k):
            return remote(source(k), target(me), send_sem.at[k], recv_sem.at[me], {axis: k})

        def copy_from(k):
            return remote(source(k), target(k), send_sem.at[k], recv_sem.at[k], {axis: k})

        def start(k, _):
            pl.when(k != me)(lambda: copy_to(k).start())
            return 0

        def arrive(k, _):
            pl.when(k != me)(lambda: copy_from(k).wait_recv())
            return 0

        def leave(k, _):
            pl.when(k != me)(lambda: copy_to(k).wait_send())
            return 0

        return tuple(lambda body=body: lax.fori_loop(0, size, body, 0) for body in (start, arrive, leave))

    start1, arrive1, leave1 = exchange(
        n_row, "row", row, lambda k: picks.at[k], lambda k: part1.at[k], p1_send, p1_recv
    )
    start2, arrive2, leave2 = exchange(n_col, "col", col, lambda k: mine, lambda k: part2.at[k], p2_send, p2_recv)
    start3, arrive3, leave3 = exchange(
        n_row, "row", row, lambda k: rtok.at[row], lambda k: rtok.at[k], p3_send, p3_recv
    )
    start1()
    part1[row] = picks[row]

    send_halo(left, own.at[0], 6, {"col": col - 1})
    send_halo(left, own.at[2], 7, {"col": col - 1})
    send_halo(right, own.at[1], 4, {"col": col + 1})
    send_halo(right, own.at[3], 5, {"col": col + 1})

    lane = lax.broadcasted_iota(jnp.int32, (1, AUG), 1)
    spare = lax.rem(lane, HDIM)
    low_half = lane < HDIM

    def query_marks(block):
        i, j = divmod(block, 2)
        marks = jnp.where(spare == 16, FAR, 0.0)
        for k in range(9):
            place = (i + k // 3, j + k % 3)
            allowed = pat_ref[block, k].astype(jnp.float32)
            exists = there(place)
            if exists is not None:
                allowed = allowed * as_int(exists).astype(jnp.float32)
            marks = jnp.where(spare == place[0] * 4 + place[1], (1.0 - allowed) * FAR, marks)
        return marks

    def key_marks(place):
        (tr, tc), (i, j) = tile_of(place)
        position = lax.broadcasted_iota(jnp.int32, (BLK, AUG), 0) + (i * 2 + j) * BLK
        beyond = jnp.where(position >= cnts[3 * tr + tc, 0:1, :], 1.0, 0.0)
        return jnp.where(spare == 16, beyond, jnp.where(spare == place[0] * 4 + place[1], 1.0, 0.0))

    def halves(pair, other):
        return jnp.where(low_half, pair, other), jnp.where(low_half, other, pair)

    def project(n, key_at, marks, part, out):
        for j in range(3):
            at = part * WIDTH + j * 256
            result = dot(normed[0:n, :], weights[:, at : at + 256]).astype(jnp.bfloat16)
            for t in range(2):
                pair = result[:, t * 128 : t * 128 + 128]
                to = j * 512 + t * 256
                first_head, second_head = halves(pair, marks)
                out[key_at : key_at + n, to : to + 128] = first_head
                out[key_at : key_at + n, to + 128 : to + 256] = second_head

    def keys_values(values, key_at, places):
        n = values.shape[0]
        normed[0:n, :] = norm_rows(values, gain_ref[...])
        if places is None:
            marks = jnp.zeros((n, AUG), jnp.bfloat16)
        else:
            marks = jnp.concatenate([key_marks(place) for place in places], axis=0).astype(jnp.bfloat16)
        project(n, key_at, marks, 1, ka)
        project(n, key_at, jnp.ones((n, AUG), jnp.bfloat16), 2, va)

    def lanes(pair, half):
        return pl.ds(pl.multiple_of(pair * (2 * AUG) + half * AUG, AUG), AUG)

    def part_of(rows, keys, at):
        def stacked(ref):
            return jnp.concatenate([ref[begin : begin + n, at] for begin, n in keys], axis=0)

        begin, n = rows
        scores = dot_t(qa[begin : begin + n, at], stacked(ka))
        probs = jnp.exp2(scores * EXP_SCALE).astype(jnp.bfloat16)
        return dot(probs, stacked(va))

    def attend_own(begin, end):
        def body(pair, _):
            for half in range(2):
                at = lanes(pair, half)
                oa[:, at] = part_of((0, OWN_KEYS), ((0, OWN_KEYS),), at)
            return 0

        lax.fori_loop(begin, end, body, 0)

    def attend_halo():
        def body(pair, _):
            for half in range(2):
                at = lanes(pair, half)
                for b in range(4):
                    i, j = divmod(b, 2)
                    groups = ((2 * i, 2), (4 + 2 * j, 2), (8 + b, 1))
                    keys = tuple((OWN_KEYS + slot * BLK, n * BLK) for slot, n in groups)
                    rows = slice(b * BLK, b * BLK + BLK)
                    oa[rows, at] += part_of((b * BLK, BLK), keys, at)
            return 0

        lax.fori_loop(0, HEADS // 2, body, 0)

    def attend_region():
        def body(pair, bad):
            one, two = (
                oa[:, lanes(pair, half)] + part_of((0, OWN_KEYS), ((REGION_AT, REGION),), lanes(pair, half))
                for half in range(2)
            )
            sums = pltpu.roll(jnp.where(low_half, two, one), HDIM, 1)
            result = jnp.where(low_half, one, two) / sums
            out_ref[:, pl.ds(pl.multiple_of(pair * AUG, AUG), AUG)] = result.astype(jnp.bfloat16)
            fine = (sums >= LOW) & (sums <= HIGH)
            return jnp.maximum(bad, jnp.max(jnp.where(fine, 0.0, 1.0), axis=0, keepdims=True))

        bad = lax.fori_loop(0, HEADS // 2, body, jnp.zeros((1, AUG), jnp.float32))
        flag_ref[0, 0] = jnp.max(bad)

    loads[1].wait()
    keys_values(tokens, 0, OWN)
    q_marks = jnp.concatenate([jnp.broadcast_to(query_marks(b), (BLK, AUG)) for b in range(4)], axis=0)
    project(OWN_KEYS, 0, q_marks.astype(jnp.bfloat16), 0, qa)

    halo_wait((0, 1, 2, 3))
    send_halo(both(up, left), halo.at[0], 9, {"col": col - 1})
    send_halo(both(up, right), halo.at[1], 8, {"col": col + 1})
    send_halo(both(down, left), halo.at[2], 11, {"col": col - 1})
    send_halo(both(down, right), halo.at[3], 10, {"col": col + 1})

    def merge(slots, number):
        total = slots[0].astype(jnp.float32)
        for k in range(1, number):
            total = total + slots[k].astype(jnp.float32)
        return total.astype(jnp.bfloat16)

    arrive1()
    mine[...] = merge(part1, n_row)
    start2()
    part2[col] = mine[...]

    attend_own(0, 3)

    arrive2()
    rtok[row] = merge(part2, n_col)
    start3()

    attend_own(3, 6)

    for exists, _, arrives in cnt_copies:
        pl.when(exists)(lambda arrives=arrives: arrives.wait_recv())
    halo_wait((4, 5, 6, 7))
    keys_values(halo[0:8].reshape(8 * BLK, WIDTH), OWN_KEYS, SLOTS[0:8])
    halo_wait((8, 9, 10, 11))
    keys_values(halo[8:12].reshape(4 * BLK, WIDTH), OWN_KEYS + 8 * BLK, SLOTS[8:12])
    attend_halo()

    arrive3()
    saves = [
        pltpu.make_async_copy(halo, halo_out, save_sem.at[0]),
        pltpu.make_async_copy(rtok, rtok_out, save_sem.at[1]),
        pltpu.make_async_copy(cnts, cnts_out, save_sem.at[2]),
    ]
    for save in saves:
        save.start()
    keys_values(rtok[...].reshape(REGION, WIDTH), REGION_AT, None)
    attend_region()

    for cond, copy in sends:
        pl.when(cond)(lambda copy=copy: copy.wait_send())
    for exists, copy, _ in cnt_copies:
        pl.when(exists)(lambda copy=copy: copy.wait_send())
    leave1()
    leave2()
    leave3()
    for save in saves:
        save.wait()


def fused(n_row, n_col, tokens, gain, w_qkv, pattern, counts, region):
    chunk = REGION // n_row
    vmem = pl.BlockSpec(memory_space=pltpu.VMEM)
    smem = pl.BlockSpec(memory_space=pltpu.SMEM)
    anywhere = pl.BlockSpec(memory_space=pl.ANY)
    bf16, f32 = jnp.bfloat16, jnp.float32
    dma = pltpu.SemaphoreType.DMA
    flops = 2 * (OWN_KEYS * WIDTH * WIDTH * 3 + (KEYS - OWN_KEYS) * WIDTH * WIDTH * 2 + OWN_KEYS * 1408 * WIDTH * 2)
    return pl.pallas_call(
        functools.partial(kernel, n_row, n_col),
        out_shape=(
            jax.ShapeDtypeStruct((OWN_KEYS, WIDTH), bf16),
            jax.ShapeDtypeStruct((1, 1), f32),
            jax.ShapeDtypeStruct((len(SLOTS), BLK, WIDTH), bf16),
            jax.ShapeDtypeStruct((n_row, chunk, WIDTH), bf16),
            jax.ShapeDtypeStruct((9, 8, 128), jnp.int32),
        ),
        in_specs=[anywhere, vmem, anywhere, smem, smem, vmem],
        out_specs=(vmem, smem, anywhere, anywhere, anywhere),
        scratch_shapes=[
            pltpu.VMEM((4, BLK, WIDTH), bf16),
            pltpu.VMEM((len(SLOTS), BLK, WIDTH), bf16),
            pltpu.VMEM((WIDTH, 3 * WIDTH), bf16),
            pltpu.VMEM((9, 8, 128), jnp.int32),
            pltpu.VMEM((n_row, chunk, WIDTH), bf16),
            pltpu.VMEM((n_row, chunk, WIDTH), bf16),
            pltpu.VMEM((chunk, WIDTH), bf16),
            pltpu.VMEM((n_col, chunk, WIDTH), bf16),
            pltpu.VMEM((n_row, chunk, WIDTH), bf16),
            pltpu.VMEM((8 * BLK, WIDTH), bf16),
            pltpu.VMEM((OWN_KEYS, HEADS * AUG), bf16),
            pltpu.VMEM((KEYS, HEADS * AUG), bf16),
            pltpu.VMEM((KEYS, HEADS * AUG), bf16),
            pltpu.VMEM((OWN_KEYS, HEADS * AUG), f32),
            dma((2,)),
            dma((12,)), dma((12,)),
            dma((9,)), dma((9,)),
            dma((n_row,)), dma((n_row,)),
            dma((n_col,)), dma((n_col,)),
            dma((n_row,)), dma((n_row,)),
            dma((3,)),
        ],
        compiler_params=pltpu.CompilerParams(
            collective_id=0, has_side_effects=True, vmem_limit_bytes=48 << 20
        ),
        cost_estimate=pl.CostEstimate(flops=flops, bytes_accessed=9 << 20, transcendentals=OWN_KEYS * 1408 * HEADS),
    )(tokens, gain, w_qkv, pattern, counts, region)


def stable(own, gain, w_qkv, pattern, row, col, n_row, n_col, halo, rtok, cnts):
    grid = {place: own[i] for i, place in enumerate(OWN)}
    grid.update({place: halo[i] for i, place in enumerate(SLOTS)})
    places = [(r, c) for r in range(4) for c in range(4)]
    rows = jnp.concatenate([grid[p] for p in places] + [rtok.reshape(REGION, WIDTH)], axis=0)
    qkv = dot(norm_rows(rows, gain), w_qkv).astype(jnp.bfloat16)
    valid = []
    for place in places:
        (tr, tc), (i, j) = tile_of(place)
        valid.append(jnp.arange(BLK) + (i * 2 + j) * BLK < cnts[3 * tr + tc, 0, 0])
    masks = []
    for block in range(4):
        i, j = divmod(block, 2)
        marks = []
        for number, (r, c) in enumerate(places):
            dr, dc = r - i, c - j
            if 0 <= dr < 3 and 0 <= dc < 3:
                a, b = row * 2 + r - 1, col * 2 + c - 1
                inside = (a >= 0) & (a < 2 * n_row) & (b >= 0) & (b < 2 * n_col)
                marks.append(valid[number] & inside & (pattern[block, 3 * dr + dc] > 0))
            else:
                marks.append(jnp.zeros((BLK,), bool))
        masks.append(jnp.concatenate(marks + [jnp.ones((REGION,), bool)]))
    mask = jnp.stack(masks)
    own_at = jnp.array([4 * r + c for r, c in OWN])
    query = qkv[: 16 * BLK, :WIDTH].reshape(16, BLK, HEADS, HDIM)[own_at]
    key = qkv[:, WIDTH : 2 * WIDTH].reshape(-1, HEADS, HDIM)
    value = qkv[:, 2 * WIDTH :].reshape(-1, HEADS, HDIM)

    def one_head(args):
        q, k, v = args
        scores = jnp.einsum("bqd,kd->bqk", q, k, preferred_element_type=jnp.float32) * (HDIM ** (-0.5))
        masked = jnp.where(mask[:, None, :], scores, -1e30)
        top = jnp.max(masked, axis=-1, keepdims=True)
        weights = jnp.where(mask[:, None, :], jnp.exp(masked - top), 0.0)
        probs = (weights / jnp.sum(weights, axis=-1, keepdims=True)).astype(jnp.bfloat16)
        return jnp.einsum("bqk,kd->bqd", probs, v, preferred_element_type=jnp.float32).astype(jnp.bfloat16)

    heads = lax.map(one_head, (query.transpose(2, 0, 1, 3), key.transpose(1, 0, 2), value.transpose(1, 0, 2)))
    joined = heads.transpose(1, 2, 0, 3).reshape(OWN_KEYS, WIDTH)
    return with_layout_constraint(joined, Layout(major_to_minor=(0, 1)))


def local(n_row, n_col, tokens, gain, w_qkv, pattern, counts, region):
    own = tokens.reshape(4, BLK, WIDTH)
    blocks = pattern.reshape(4, 9)
    scale = gain.reshape(1, WIDTH)
    out, flag, halo, rtok, cnts = fused(
        n_row, n_col, own, scale, w_qkv, blocks, counts, region.reshape(1, REGION)
    )
    row, col = lax.axis_index("row"), lax.axis_index("col")
    result = lax.cond(
        flag[0, 0] > 0.0,
        lambda: stable(own, scale, w_qkv, blocks, row, col, n_row, n_col, halo, rtok, cnts),
        lambda: out,
    )
    live = jnp.arange(OWN_KEYS, dtype=jnp.int32) < counts[0, 0]
    return jnp.where(live[:, None], result, jnp.zeros_like(result)).reshape(tokens.shape)


def solution(mesh):
    in_specs = (
        P(("scan", "row"), "col", None, None, None, None),
        P(),
        P(),
        P(("scan", "row"), "col", None, None, None),
        P(("scan", "row"), "col"),
        P("scan"),
    )
    out_specs = P(("scan", "row"), "col", None, None, None, None)
    body = functools.partial(local, mesh.shape["row"], mesh.shape["col"])
    return jax.shard_map(body, mesh=mesh, in_specs=in_specs, out_specs=out_specs, check_vma=False)
```

```python
import functools

import jax
import jax.numpy as jnp
from jax import lax
from jax.experimental import pallas as pl
from jax.experimental.layout import Layout, with_layout_constraint
from jax.experimental.pallas import tpu as pltpu
from jax.sharding import PartitionSpec as P

HEADS = 12
HDIM = 64
BLK = 128
WIDTH = HEADS * HDIM
AUG = 2 * HDIM
REGION = 256
MESH = pl.DeviceIdType.MESH
EXP_SCALE = (HDIM ** (-0.5)) * 1.4426950408889634
FAR = -1e30
LOW, HIGH = 2.0 ** (-80), 2.0**100

SLOTS = ((0, 1), (0, 2), (3, 1), (3, 2), (1, 0), (2, 0), (1, 3), (2, 3), (0, 0), (0, 3), (3, 0), (3, 3))
OWN = ((1, 1), (1, 2), (2, 1), (2, 2))
OWN_KEYS = 4 * BLK
HALO_KEYS = len(SLOTS) * BLK
REGION_AT = OWN_KEYS + HALO_KEYS
KEYS = REGION_AT + REGION


def dot(a, b):
    return lax.dot_general(a, b, (((1,), (0,)), ((), ())), preferred_element_type=jnp.float32)


def dot_t(a, b):
    return lax.dot_general(a, b, (((1,), (1,)), ((), ())), preferred_element_type=jnp.float32)


def norm_rows(values, gain):
    floats = values.astype(jnp.float32)
    center = floats - jnp.sum(floats, axis=-1, keepdims=True) * (1.0 / WIDTH)
    spread = jnp.sum(center * center, axis=-1, keepdims=True) * (1.0 / WIDTH)
    return (center * lax.rsqrt(spread + 1e-05) * gain).astype(jnp.bfloat16)


def tile_of(place):
    return tuple((0, 1, 1, 2)[p] for p in place), tuple((1, 0, 1, 0)[p] for p in place)


def kernel(
    n_row, n_col,
    tok_hbm, gain_hbm, w_hbm, pat_ref, cnt_ref, reg_hbm,
    out_ref, flag_ref, halo_out, rtok_out, cnts_out,
    own, halo, weights, cnts, picks, part1, mine, part2, rtok, normed, qa, ka, va, oa, gain_ref, reg_ref,
    load_sem, halo_send, halo_recv, cnt_send, cnt_recv, p1_send, p1_recv, p2_send, p2_recv, p3_send, p3_recv, save_sem,
):
    row, col = lax.axis_index("row"), lax.axis_index("col")
    up, down, left, right = row > 0, row < n_row - 1, col > 0, col < n_col - 1
    exists_r, exists_c = (up, None, None, down), (left, None, None, right)
    chunk = REGION // n_row

    def both(a, b):
        return b if a is None else (a if b is None else a & b)

    def there(place):
        return both(exists_r[place[0]], exists_c[place[1]])

    loads = [
        pltpu.make_async_copy(tok_hbm, own, load_sem.at[0]),
        pltpu.make_async_copy(w_hbm, weights, load_sem.at[1]),
        pltpu.make_async_copy(gain_hbm, gain_ref, load_sem.at[2]),
        pltpu.make_async_copy(reg_hbm, reg_ref, load_sem.at[3]),
    ]
    for load in loads:
        load.start()

    barrier = pltpu.get_barrier_semaphore()
    diagonals = [(dr, dc) for dr in (-1, 1) for dc in (-1, 1)]

    def signal_row(r, _):
        @pl.when(r != row)
        def _():
            pl.semaphore_signal(barrier, inc=1, device_id={"row": r}, device_id_type=MESH)
        return 0

    def signal_col(c, _):
        @pl.when(c != col)
        def _():
            pl.semaphore_signal(barrier, inc=1, device_id={"col": c}, device_id_type=MESH)
        return 0

    lax.fori_loop(0, n_row, signal_row, 0)
    lax.fori_loop(0, n_col, signal_col, 0)
    for dr, dc in diagonals:
        @pl.when(both(up if dr < 0 else down, left if dc < 0 else right))
        def _(dr=dr, dc=dc):
            pl.semaphore_signal(barrier, inc=1, device_id={"row": row + dr, "col": col + dc}, device_id_type=MESH)

    as_int = lambda flag: jnp.where(flag, 1, 0)
    n_diag = (as_int(up) + as_int(down)) * (as_int(left) + as_int(right))

    for group in range(4):
        @pl.when(jnp.logical_not((up, down, left, right)[group]))
        def _(group=group):
            halo[2 * group : 2 * group + 2] = jnp.zeros((2, BLK, WIDTH), jnp.bfloat16)
    for slot in range(8, 12):
        @pl.when(jnp.logical_not(there(SLOTS[slot])))
        def _(slot=slot):
            halo[slot] = jnp.zeros((BLK, WIDTH), jnp.bfloat16)
    count = cnt_ref[0, 0]
    for t in range(9):
        if t == 4:
            cnts[t] = jnp.broadcast_to(count, (8, 128)).astype(jnp.int32)
        else:
            dr, dc = t // 3 - 1, t % 3 - 1
            exists = both((up, None, down)[dr + 1], (left, None, right)[dc + 1])

            @pl.when(jnp.logical_not(exists))
            def _(t=t):
                cnts[t] = jnp.zeros((8, 128), jnp.int32)

    loads[0].wait()
    loads[2].wait()
    loads[3].wait()

    tokens = own[...].reshape(OWN_KEYS, WIDTH)
    first = (row * n_col + col) * OWN_KEYS
    flat = lax.broadcasted_iota(jnp.int32, (OWN_KEYS, REGION), 0) + first
    hit = jnp.where(flat == reg_ref[...][None, :], 1.0, 0.0).astype(jnp.bfloat16)
    found = lax.dot_general(hit, tokens, (((0,), (0,)), ((), ())), preferred_element_type=jnp.float32)
    picks[...] = found.astype(jnp.bfloat16).reshape(n_row, chunk, WIDTH)

    pl.semaphore_wait(barrier, n_row + n_col - 2 + n_diag)

    def remote(src, dst, send, recv, device):
        return pltpu.make_async_remote_copy(
            src_ref=src, dst_ref=dst, send_sem=send, recv_sem=recv, device_id=device, device_id_type=MESH
        )

    sends = []

    def send_halo(cond, src, slot, device):
        copy = remote(src, halo.at[slot], halo_send.at[len(sends)], halo_recv.at[slot], device)
        sends.append((cond, copy))
        pl.when(cond)(lambda: copy.start())

    def halo_wait(slots):
        for slot in slots:
            copy = remote(halo.at[slot], halo.at[slot], halo_send.at[slot], halo_recv.at[slot], {"row": row})
            pl.when(there(SLOTS[slot]))(lambda copy=copy: copy.wait_recv())

    cnt_copies = []
    for t in range(9):
        if t != 4:
            dr, dc = t // 3 - 1, t % 3 - 1
            exists = both((up, None, down)[dr + 1], (left, None, right)[dc + 1])
            device = {}
            if dr:
                device["row"] = row + dr
            if dc:
                device["col"] = col + dc
            copy = remote(cnts.at[4], cnts.at[8 - t], cnt_send.at[t], cnt_recv.at[8 - t], device)
            arrives = remote(cnts.at[4], cnts.at[t], cnt_send.at[t], cnt_recv.at[t], device)
            cnt_copies.append((exists, copy, arrives))
            pl.when(exists)(lambda copy=copy: copy.start())

    def exchange(size, axis, me, source, target, send_sem, recv_sem):
        def copy_to(k):
            return remote(source(k), target(me), send_sem.at[k], recv_sem.at[me], {axis: k})

        def copy_from(k):
            return remote(source(k), target(k), send_sem.at[k], recv_sem.at[k], {axis: k})

        def start(k, _):
            pl.when(k != me)(lambda: copy_to(k).start())
            return 0

        def arrive(k, _):
            pl.when(k != me)(lambda: copy_from(k).wait_recv())
            return 0

        def leave(k, _):
            pl.when(k != me)(lambda: copy_to(k).wait_send())
            return 0

        return tuple(lambda body=body: lax.fori_loop(0, size, body, 0) for body in (start, arrive, leave))

    start1, arrive1, leave1 = exchange(
        n_row, "row", row, lambda k: picks.at[k], lambda k: part1.at[k], p1_send, p1_recv
    )
    start2, arrive2, leave2 = exchange(n_col, "col", col, lambda k: mine, lambda k: part2.at[k], p2_send, p2_recv)
    start3, arrive3, leave3 = exchange(
        n_row, "row", row, lambda k: rtok.at[row], lambda k: rtok.at[k], p3_send, p3_recv
    )
    start1()
    part1[row] = picks[row]

    send_halo(up, own.at[0], 2, {"row": row - 1})
    send_halo(up, own.at[1], 3, {"row": row - 1})
    send_halo(down, own.at[2], 0, {"row": row + 1})
    send_halo(down, own.at[3], 1, {"row": row + 1})

    lane = lax.broadcasted_iota(jnp.int32, (1, AUG), 1)
    spare = lax.rem(lane, HDIM)
    low_half = lane < HDIM

    def query_marks(block):
        i, j = divmod(block, 2)
        marks = jnp.where(spare <= 16, FAR, 0.0)
        for k in range(9):
            place = (i + k // 3, j + k % 3)
            allowed = pat_ref[block, k].astype(jnp.float32)
            exists = there(place)
            if exists is not None:
                allowed = allowed * as_int(exists).astype(jnp.float32)
            marks = jnp.where(spare == place[0] * 4 + place[1], (1.0 - allowed) * FAR, marks)
        return marks

    def key_marks(place):
        (tr, tc), (i, j) = tile_of(place)
        position = lax.broadcasted_iota(jnp.int32, (BLK, AUG), 0) + (i * 2 + j) * BLK
        beyond = jnp.where(position >= cnts[3 * tr + tc, 0:1, :], 1.0, 0.0)
        return jnp.where(spare == 16, beyond, jnp.where(spare == place[0] * 4 + place[1], 1.0, 0.0))

    def halves(pair, other):
        return jnp.where(low_half, pair, other), jnp.where(low_half, other, pair)

    def project(n, key_at, marks, part, out):
        for j in range(3):
            at = part * WIDTH + j * 256
            result = dot(normed[0:n, :], weights[:, at : at + 256]).astype(jnp.bfloat16)
            for t in range(2):
                pair = result[:, t * 128 : t * 128 + 128]
                to = j * 512 + t * 256
                first_head, second_head = halves(pair, marks)
                out[key_at : key_at + n, to : to + 128] = first_head
                out[key_at : key_at + n, to + 128 : to + 256] = second_head

    def keys_values(values, key_at, places):
        n = values.shape[0]
        normed[0:n, :] = norm_rows(values, gain_ref[...][None, :])
        if places is None:
            marks = jnp.zeros((n, AUG), jnp.bfloat16)
        else:
            marks = jnp.concatenate([key_marks(place) for place in places], axis=0).astype(jnp.bfloat16)
        project(n, key_at, marks, 1, ka)
        project(n, key_at, jnp.ones((n, AUG), jnp.bfloat16), 2, va)

    def lanes(pair, half):
        return pl.ds(pl.multiple_of(pair * (2 * AUG) + half * AUG, AUG), AUG)

    def part_of(blocks, keys, at):
        def stacked(ref, groups):
            return jnp.concatenate([ref[begin : begin + n, at] for begin, n in groups], axis=0)

        scores = dot_t(stacked(qa, [(b * BLK, BLK) for b in blocks]), stacked(ka, keys))
        probs = jnp.exp2(scores * EXP_SCALE).astype(jnp.bfloat16)
        return dot(probs, stacked(va, keys))

    def attend_own(begin, end):
        def body(pair, _):
            for half in range(2):
                at = lanes(pair, half)
                oa[:, at] = part_of(range(4), ((0, OWN_KEYS),), at)
            return 0

        lax.fori_loop(begin, end, body, 0)

    def slots_at(*groups):
        return tuple((OWN_KEYS + slot * BLK, n * BLK) for slot, n in groups)

    def attend_halo():
        def body(pair, _):
            for half in range(2):
                at = lanes(pair, half)
                above = part_of((0, 1), slots_at((0, 2), (8, 2)), at)
                below = part_of((2, 3), slots_at((2, 2), (10, 2)), at)
                before = part_of((0, 2), slots_at((4, 2)), at)
                after = part_of((1, 3), slots_at((6, 2)), at)
                for b in range(4):
                    i, j = divmod(b, 2)
                    vertical = (below if i else above)[j * BLK : j * BLK + BLK]
                    horizontal = (after if j else before)[i * BLK : i * BLK + BLK]
                    oa[b * BLK : b * BLK + BLK, at] += vertical + horizontal
            return 0

        lax.fori_loop(0, HEADS // 2, body, 0)

    def attend_region():
        def body(pair, bad):
            one, two = (
                oa[:, lanes(pair, half)] + part_of(range(4), ((REGION_AT, REGION),), lanes(pair, half))
                for half in range(2)
            )
            sums = pltpu.roll(jnp.where(low_half, two, one), HDIM, 1)
            result = jnp.where(low_half, one, two) / sums
            out_ref[:, pl.ds(pl.multiple_of(pair * AUG, AUG), AUG)] = result.astype(jnp.bfloat16)
            fine = (sums >= LOW) & (sums <= HIGH)
            return jnp.maximum(bad, jnp.max(jnp.where(fine, 0.0, 1.0), axis=0, keepdims=True))

        bad = lax.fori_loop(0, HEADS // 2, body, jnp.zeros((1, AUG), jnp.float32))
        flag_ref[0, 0] = jnp.max(bad)

    loads[1].wait()
    keys_values(tokens, 0, OWN)
    q_marks = jnp.concatenate([jnp.broadcast_to(query_marks(b), (BLK, AUG)) for b in range(4)], axis=0)
    project(OWN_KEYS, 0, q_marks.astype(jnp.bfloat16), 0, qa)

    def merge(slots, number):
        total = slots[0].astype(jnp.float32)
        for k in range(1, number):
            total = total + slots[k].astype(jnp.float32)
        return total.astype(jnp.bfloat16)

    attend_own(0, 2)

    arrive1()
    mine[...] = merge(part1, n_row)
    start2()
    part2[col] = mine[...]

    send_halo(left, own.at[0], 6, {"col": col - 1})
    send_halo(left, own.at[2], 7, {"col": col - 1})
    send_halo(right, own.at[1], 4, {"col": col + 1})
    send_halo(right, own.at[3], 5, {"col": col + 1})
    halo_wait((0, 1, 2, 3))
    send_halo(both(up, left), halo.at[0], 9, {"col": col - 1})
    send_halo(both(up, right), halo.at[1], 8, {"col": col + 1})
    send_halo(both(down, left), halo.at[2], 11, {"col": col - 1})
    send_halo(both(down, right), halo.at[3], 10, {"col": col + 1})

    attend_own(2, 4)

    arrive2()
    rtok[row] = merge(part2, n_col)
    start3()

    attend_own(4, 6)

    for exists, _, arrives in cnt_copies:
        pl.when(exists)(lambda arrives=arrives: arrives.wait_recv())
    halo_wait((4, 5, 6, 7))
    keys_values(halo[0:8].reshape(8 * BLK, WIDTH), OWN_KEYS, SLOTS[0:8])
    halo_wait((8, 9, 10, 11))
    keys_values(halo[8:12].reshape(4 * BLK, WIDTH), OWN_KEYS + 8 * BLK, SLOTS[8:12])
    attend_halo()

    arrive3()
    saves = [
        pltpu.make_async_copy(halo, halo_out, save_sem.at[0]),
        pltpu.make_async_copy(rtok, rtok_out, save_sem.at[1]),
        pltpu.make_async_copy(cnts, cnts_out, save_sem.at[2]),
    ]
    for save in saves:
        save.start()
    keys_values(rtok[...].reshape(REGION, WIDTH), REGION_AT, None)
    attend_region()

    for cond, copy in sends:
        pl.when(cond)(lambda copy=copy: copy.wait_send())
    for exists, copy, _ in cnt_copies:
        pl.when(exists)(lambda copy=copy: copy.wait_send())
    leave1()
    leave2()
    leave3()
    for save in saves:
        save.wait()


def fused(n_row, n_col, tokens, gain, w_qkv, pattern, counts, region):
    chunk = REGION // n_row
    vmem = pl.BlockSpec(memory_space=pltpu.VMEM)
    smem = pl.BlockSpec(memory_space=pltpu.SMEM)
    anywhere = pl.BlockSpec(memory_space=pl.ANY)
    hbm = pl.BlockSpec(memory_space=pltpu.HBM)
    bf16, f32 = jnp.bfloat16, jnp.float32
    dma = pltpu.SemaphoreType.DMA
    flops = 2 * (OWN_KEYS * WIDTH * WIDTH * 3 + (KEYS - OWN_KEYS) * WIDTH * WIDTH * 2 + OWN_KEYS * 1408 * WIDTH * 2)
    return pl.pallas_call(
        functools.partial(kernel, n_row, n_col),
        out_shape=(
            pltpu.VMEM((OWN_KEYS, WIDTH), bf16),
            jax.ShapeDtypeStruct((1, 1), f32),
            jax.ShapeDtypeStruct((len(SLOTS), BLK, WIDTH), bf16),
            jax.ShapeDtypeStruct((n_row, chunk, WIDTH), bf16),
            jax.ShapeDtypeStruct((9, 8, 128), jnp.int32),
        ),
        in_specs=[hbm, hbm, hbm, smem, smem, hbm],
        out_specs=(vmem, smem, anywhere, anywhere, anywhere),
        scratch_shapes=[
            pltpu.VMEM((4, BLK, WIDTH), bf16),
            pltpu.VMEM((len(SLOTS), BLK, WIDTH), bf16),
            pltpu.VMEM((WIDTH, 3 * WIDTH), bf16),
            pltpu.VMEM((9, 8, 128), jnp.int32),
            pltpu.VMEM((n_row, chunk, WIDTH), bf16),
            pltpu.VMEM((n_row, chunk, WIDTH), bf16),
            pltpu.VMEM((chunk, WIDTH), bf16),
            pltpu.VMEM((n_col, chunk, WIDTH), bf16),
            pltpu.VMEM((n_row, chunk, WIDTH), bf16),
            pltpu.VMEM((8 * BLK, WIDTH), bf16),
            pltpu.VMEM((OWN_KEYS, HEADS * AUG), bf16),
            pltpu.VMEM((KEYS, HEADS * AUG), bf16),
            pltpu.VMEM((KEYS, HEADS * AUG), bf16),
            pltpu.VMEM((OWN_KEYS, HEADS * AUG), f32),
            pltpu.VMEM((WIDTH,), f32),
            pltpu.VMEM((REGION,), jnp.int32),
            dma((4,)),
            dma((12,)), dma((12,)),
            dma((9,)), dma((9,)),
            dma((n_row,)), dma((n_row,)),
            dma((n_col,)), dma((n_col,)),
            dma((n_row,)), dma((n_row,)),
            dma((3,)),
        ],
        compiler_params=pltpu.CompilerParams(
            collective_id=0, has_side_effects=True, vmem_limit_bytes=48 << 20
        ),
        cost_estimate=pl.CostEstimate(flops=flops, bytes_accessed=9 << 20, transcendentals=OWN_KEYS * 1408 * HEADS),
    )(tokens, gain, w_qkv, pattern, counts, region)


def stable(own, gain, w_qkv, pattern, row, col, n_row, n_col, halo, rtok, cnts):
    grid = {place: own[i] for i, place in enumerate(OWN)}
    grid.update({place: halo[i] for i, place in enumerate(SLOTS)})
    places = [(r, c) for r in range(4) for c in range(4)]
    rows = jnp.concatenate([grid[p] for p in places] + [rtok.reshape(REGION, WIDTH)], axis=0)
    qkv = dot(norm_rows(rows, gain), w_qkv).astype(jnp.bfloat16)
    valid = []
    for place in places:
        (tr, tc), (i, j) = tile_of(place)
        valid.append(jnp.arange(BLK) + (i * 2 + j) * BLK < cnts[3 * tr + tc, 0, 0])
    masks = []
    for block in range(4):
        i, j = divmod(block, 2)
        marks = []
        for number, (r, c) in enumerate(places):
            dr, dc = r - i, c - j
            if 0 <= dr < 3 and 0 <= dc < 3:
                a, b = row * 2 + r - 1, col * 2 + c - 1
                inside = (a >= 0) & (a < 2 * n_row) & (b >= 0) & (b < 2 * n_col)
                marks.append(valid[number] & inside & (pattern[block, 3 * dr + dc] > 0))
            else:
                marks.append(jnp.zeros((BLK,), bool))
        masks.append(jnp.concatenate(marks + [jnp.ones((REGION,), bool)]))
    mask = jnp.stack(masks)
    own_at = jnp.array([4 * r + c for r, c in OWN])
    query = qkv[: 16 * BLK, :WIDTH].reshape(16, BLK, HEADS, HDIM)[own_at]
    key = qkv[:, WIDTH : 2 * WIDTH].reshape(-1, HEADS, HDIM)
    value = qkv[:, 2 * WIDTH :].reshape(-1, HEADS, HDIM)

    def one_head(args):
        q, k, v = args
        scores = jnp.einsum("bqd,kd->bqk", q, k, preferred_element_type=jnp.float32) * (HDIM ** (-0.5))
        masked = jnp.where(mask[:, None, :], scores, -1e30)
        top = jnp.max(masked, axis=-1, keepdims=True)
        weights = jnp.where(mask[:, None, :], jnp.exp(masked - top), 0.0)
        probs = (weights / jnp.sum(weights, axis=-1, keepdims=True)).astype(jnp.bfloat16)
        return jnp.einsum("bqk,kd->bqd", probs, v, preferred_element_type=jnp.float32).astype(jnp.bfloat16)

    heads = lax.map(one_head, (query.transpose(2, 0, 1, 3), key.transpose(1, 0, 2), value.transpose(1, 0, 2)))
    joined = heads.transpose(1, 2, 0, 3).reshape(OWN_KEYS, WIDTH)
    return with_layout_constraint(joined, Layout(major_to_minor=(0, 1)))


def local(n_row, n_col, tokens, gain, w_qkv, pattern, counts, region):
    own = tokens.reshape(4, BLK, WIDTH)
    blocks = pattern.reshape(4, 9)
    out, flag, halo, rtok, cnts = fused(
        n_row, n_col, own, gain, w_qkv, blocks, counts, region
    )
    row, col = lax.axis_index("row"), lax.axis_index("col")
    result = lax.cond(
        flag[0, 0] > 0.0,
        lambda: stable(own, gain.reshape(1, WIDTH), w_qkv, blocks, row, col, n_row, n_col, halo, rtok, cnts),
        lambda: out,
    )
    live = jnp.arange(OWN_KEYS, dtype=jnp.int32) < counts[0, 0]
    return jnp.where(live[:, None], result, jnp.zeros_like(result)).reshape(tokens.shape)


def solution(mesh):
    in_specs = (
        P(("scan", "row"), "col", None, None, None, None),
        P(),
        P(),
        P(("scan", "row"), "col", None, None, None),
        P(("scan", "row"), "col"),
        P("scan"),
    )
    out_specs = P(("scan", "row"), "col", None, None, None, None)
    body = functools.partial(local, mesh.shape["row"], mesh.shape["col"])
    return jax.shard_map(body, mesh=mesh, in_specs=in_specs, out_specs=out_specs, check_vma=False)
```

```python
import functools

import jax
import jax.numpy as jnp
from jax import lax
from jax.experimental import pallas as pl
from jax.experimental.layout import Layout, with_layout_constraint
from jax.experimental.pallas import tpu as pltpu
from jax.sharding import PartitionSpec as P

HEADS = 12
HDIM = 64
BLK = 128
WIDTH = HEADS * HDIM
AUG = 2 * HDIM
REGION = 256
MESH = pl.DeviceIdType.MESH
EXP_SCALE = (HDIM ** (-0.5)) * 1.4426950408889634
FAR = -1e30
LOW, HIGH = 2.0 ** (-80), 2.0**100

SLOTS = ((0, 1), (0, 2), (3, 1), (3, 2), (1, 0), (2, 0), (1, 3), (2, 3), (0, 0), (0, 3), (3, 0), (3, 3))
OWN = ((1, 1), (1, 2), (2, 1), (2, 2))
OWN_KEYS = 4 * BLK
HALO_KEYS = len(SLOTS) * BLK
REGION_AT = OWN_KEYS + HALO_KEYS
KEYS = REGION_AT + REGION


def dot(a, b):
    return lax.dot_general(a, b, (((1,), (0,)), ((), ())), preferred_element_type=jnp.float32)


def dot_t(a, b):
    return lax.dot_general(a, b, (((1,), (1,)), ((), ())), preferred_element_type=jnp.float32)


def norm_rows(values, gain):
    floats = values.astype(jnp.float32)
    center = floats - jnp.sum(floats, axis=-1, keepdims=True) * (1.0 / WIDTH)
    spread = jnp.sum(center * center, axis=-1, keepdims=True) * (1.0 / WIDTH)
    return (center * lax.rsqrt(spread + 1e-05) * gain).astype(jnp.bfloat16)


def tile_of(place):
    return tuple((0, 1, 1, 2)[p] for p in place), tuple((1, 0, 1, 0)[p] for p in place)


def kernel(
    n_row, n_col,
    tok_hbm, gain_hbm, w_hbm, pat_ref, cnt_ref, reg_hbm,
    out_ref, flag_ref, halo_out, rtok_out, cnts_out,
    own, halo, weights, cnts, picks, part1, mine, part2, rtok, normed, qa, ka, va, oa, gain_ref, reg_ref,
    load_sem, halo_send, halo_recv, cnt_send, cnt_recv, p1_send, p1_recv, p2_send, p2_recv, p3_send, p3_recv, save_sem,
):
    row, col = lax.axis_index("row"), lax.axis_index("col")
    up, down, left, right = row > 0, row < n_row - 1, col > 0, col < n_col - 1
    exists_r, exists_c = (up, None, None, down), (left, None, None, right)
    chunk = REGION // n_row

    def both(a, b):
        return b if a is None else (a if b is None else a & b)

    def there(place):
        return both(exists_r[place[0]], exists_c[place[1]])

    loads = [
        pltpu.make_async_copy(tok_hbm, own, load_sem.at[0]),
        pltpu.make_async_copy(w_hbm, weights, load_sem.at[1]),
        pltpu.make_async_copy(gain_hbm, gain_ref, load_sem.at[2]),
        pltpu.make_async_copy(reg_hbm, reg_ref, load_sem.at[3]),
    ]
    for load in loads:
        load.start()

    barrier = pltpu.get_barrier_semaphore()
    diagonals = [(dr, dc) for dr in (-1, 1) for dc in (-1, 1)]

    def signal_row(r, _):
        @pl.when(r != row)
        def _():
            pl.semaphore_signal(barrier, inc=1, device_id={"row": r}, device_id_type=MESH)
        return 0

    def signal_col(c, _):
        @pl.when(c != col)
        def _():
            pl.semaphore_signal(barrier, inc=1, device_id={"col": c}, device_id_type=MESH)
        return 0

    lax.fori_loop(0, n_row, signal_row, 0)
    lax.fori_loop(0, n_col, signal_col, 0)
    for dr, dc in diagonals:
        @pl.when(both(up if dr < 0 else down, left if dc < 0 else right))
        def _(dr=dr, dc=dc):
            pl.semaphore_signal(barrier, inc=1, device_id={"row": row + dr, "col": col + dc}, device_id_type=MESH)

    as_int = lambda flag: jnp.where(flag, 1, 0)
    n_diag = (as_int(up) + as_int(down)) * (as_int(left) + as_int(right))

    for group in range(4):
        @pl.when(jnp.logical_not((up, down, left, right)[group]))
        def _(group=group):
            halo[2 * group : 2 * group + 2] = jnp.zeros((2, BLK, WIDTH), jnp.bfloat16)
    for slot in range(8, 12):
        @pl.when(jnp.logical_not(there(SLOTS[slot])))
        def _(slot=slot):
            halo[slot] = jnp.zeros((BLK, WIDTH), jnp.bfloat16)
    count = cnt_ref[0, 0]
    for t in range(9):
        if t == 4:
            cnts[t] = jnp.broadcast_to(count, (8, 128)).astype(jnp.int32)
        else:
            dr, dc = t // 3 - 1, t % 3 - 1
            exists = both((up, None, down)[dr + 1], (left, None, right)[dc + 1])

            @pl.when(jnp.logical_not(exists))
            def _(t=t):
                cnts[t] = jnp.zeros((8, 128), jnp.int32)

    loads[0].wait()
    loads[2].wait()
    loads[3].wait()

    tokens = own[...].reshape(OWN_KEYS, WIDTH)
    first = (row * n_col + col) * OWN_KEYS
    flat = lax.broadcasted_iota(jnp.int32, (OWN_KEYS, REGION), 0) + first
    hit = jnp.where(flat == reg_ref[...][None, :], 1.0, 0.0).astype(jnp.bfloat16)
    found = lax.dot_general(hit, tokens, (((0,), (0,)), ((), ())), preferred_element_type=jnp.float32)
    picks[...] = found.astype(jnp.bfloat16).reshape(n_row, chunk, WIDTH)

    pl.semaphore_wait(barrier, n_row + n_col - 2 + n_diag)

    def remote(src, dst, send, recv, device):
        return pltpu.make_async_remote_copy(
            src_ref=src, dst_ref=dst, send_sem=send, recv_sem=recv, device_id=device, device_id_type=MESH
        )

    sends = []

    def send_halo(cond, src, slot, device):
        copy = remote(src, halo.at[slot], halo_send.at[len(sends)], halo_recv.at[slot], device)
        sends.append((cond, copy))
        pl.when(cond)(lambda: copy.start())

    def halo_wait(slots):
        for slot in slots:
            copy = remote(halo.at[slot], halo.at[slot], halo_send.at[slot], halo_recv.at[slot], {"row": row})
            pl.when(there(SLOTS[slot]))(lambda copy=copy: copy.wait_recv())

    cnt_copies = []
    for t in range(9):
        if t != 4:
            dr, dc = t // 3 - 1, t % 3 - 1
            exists = both((up, None, down)[dr + 1], (left, None, right)[dc + 1])
            device = {}
            if dr:
                device["row"] = row + dr
            if dc:
                device["col"] = col + dc
            copy = remote(cnts.at[4], cnts.at[8 - t], cnt_send.at[t], cnt_recv.at[8 - t], device)
            arrives = remote(cnts.at[4], cnts.at[t], cnt_send.at[t], cnt_recv.at[t], device)
            cnt_copies.append((exists, copy, arrives))
            pl.when(exists)(lambda copy=copy: copy.start())

    def exchange(size, axis, me, source, target, send_sem, recv_sem):
        def copy_to(k):
            return remote(source(k), target(me), send_sem.at[k], recv_sem.at[me], {axis: k})

        def copy_from(k):
            return remote(source(k), target(k), send_sem.at[k], recv_sem.at[k], {axis: k})

        def start(k, _):
            pl.when(k != me)(lambda: copy_to(k).start())
            return 0

        def arrive(k, _):
            pl.when(k != me)(lambda: copy_from(k).wait_recv())
            return 0

        def leave(k, _):
            pl.when(k != me)(lambda: copy_to(k).wait_send())
            return 0

        return tuple(lambda body=body: lax.fori_loop(0, size, body, 0) for body in (start, arrive, leave))

    start1, arrive1, leave1 = exchange(
        n_row, "row", row, lambda k: picks.at[k], lambda k: part1.at[k], p1_send, p1_recv
    )
    start2, arrive2, leave2 = exchange(n_col, "col", col, lambda k: mine, lambda k: part2.at[k], p2_send, p2_recv)
    start3, arrive3, leave3 = exchange(
        n_row, "row", row, lambda k: rtok.at[row], lambda k: rtok.at[k], p3_send, p3_recv
    )
    send_halo(up, own.at[0], 2, {"row": row - 1})
    send_halo(up, own.at[1], 3, {"row": row - 1})
    send_halo(down, own.at[2], 0, {"row": row + 1})
    send_halo(down, own.at[3], 1, {"row": row + 1})

    start1()
    part1[row] = picks[row]

    send_halo(left, own.at[0], 6, {"col": col - 1})
    send_halo(left, own.at[2], 7, {"col": col - 1})
    send_halo(right, own.at[1], 4, {"col": col + 1})
    send_halo(right, own.at[3], 5, {"col": col + 1})

    lane = lax.broadcasted_iota(jnp.int32, (1, AUG), 1)
    spare = lax.rem(lane, HDIM)
    low_half = lane < HDIM

    def query_marks(block):
        i, j = divmod(block, 2)
        marks = jnp.where(spare <= 16, FAR, 0.0)
        for k in range(9):
            place = (i + k // 3, j + k % 3)
            allowed = pat_ref[block, k].astype(jnp.float32)
            exists = there(place)
            if exists is not None:
                allowed = allowed * as_int(exists).astype(jnp.float32)
            marks = jnp.where(spare == place[0] * 4 + place[1], (1.0 - allowed) * FAR, marks)
        return marks

    def key_marks(place):
        (tr, tc), (i, j) = tile_of(place)
        position = lax.broadcasted_iota(jnp.int32, (BLK, AUG), 0) + (i * 2 + j) * BLK
        beyond = jnp.where(position >= cnts[3 * tr + tc, 0:1, :], 1.0, 0.0)
        return jnp.where(spare == 16, beyond, jnp.where(spare == place[0] * 4 + place[1], 1.0, 0.0))

    def halves(pair, other):
        return jnp.where(low_half, pair, other), jnp.where(low_half, other, pair)

    def project(n, key_at, marks, part, out):
        for j in range(3):
            at = part * WIDTH + j * 256
            result = dot(normed[0:n, :], weights[:, at : at + 256]).astype(jnp.bfloat16)
            for t in range(2):
                pair = result[:, t * 128 : t * 128 + 128]
                to = j * 512 + t * 256
                first_head, second_head = halves(pair, marks)
                out[key_at : key_at + n, to : to + 128] = first_head
                out[key_at : key_at + n, to + 128 : to + 256] = second_head

    def keys_values(values, key_at, places):
        n = values.shape[0]
        normed[0:n, :] = norm_rows(values, gain_ref[...][None, :])
        if places is None:
            marks = jnp.zeros((n, AUG), jnp.bfloat16)
        else:
            marks = jnp.concatenate([key_marks(place) for place in places], axis=0).astype(jnp.bfloat16)
        project(n, key_at, marks, 1, ka)
        project(n, key_at, jnp.ones((n, AUG), jnp.bfloat16), 2, va)

    def lanes(pair, half):
        return pl.ds(pl.multiple_of(pair * (2 * AUG) + half * AUG, AUG), AUG)

    def part_of(blocks, keys, at):
        def stacked(ref, groups):
            return jnp.concatenate([ref[begin : begin + n, at] for begin, n in groups], axis=0)

        scores = dot_t(stacked(qa, [(b * BLK, BLK) for b in blocks]), stacked(ka, keys))
        probs = jnp.exp2(scores * EXP_SCALE).astype(jnp.bfloat16)
        return dot(probs, stacked(va, keys))

    def attend_own(begin, end):
        def body(pair, _):
            for half in range(2):
                at = lanes(pair, half)
                oa[:, at] = part_of(range(4), ((0, OWN_KEYS),), at)
            return 0

        lax.fori_loop(begin, end, body, 0)

    def slots_at(*groups):
        return tuple((OWN_KEYS + slot * BLK, n * BLK) for slot, n in groups)

    def attend_halo():
        def body(pair, _):
            for half in range(2):
                at = lanes(pair, half)
                above = part_of((0, 1), slots_at((0, 2), (8, 2)), at)
                below = part_of((2, 3), slots_at((2, 2), (10, 2)), at)
                before = part_of((0, 2), slots_at((4, 2)), at)
                after = part_of((1, 3), slots_at((6, 2)), at)
                for b in range(4):
                    i, j = divmod(b, 2)
                    vertical = (below if i else above)[j * BLK : j * BLK + BLK]
                    horizontal = (after if j else before)[i * BLK : i * BLK + BLK]
                    oa[b * BLK : b * BLK + BLK, at] += vertical + horizontal
            return 0

        lax.fori_loop(0, HEADS // 2, body, 0)

    def attend_region():
        def body(pair, bad):
            one, two = (
                oa[:, lanes(pair, half)] + part_of(range(4), ((REGION_AT, REGION),), lanes(pair, half))
                for half in range(2)
            )
            sums = pltpu.roll(jnp.where(low_half, two, one), HDIM, 1)
            result = jnp.where(low_half, one, two) / sums
            out_ref[:, pl.ds(pl.multiple_of(pair * AUG, AUG), AUG)] = result.astype(jnp.bfloat16)
            fine = (sums >= LOW) & (sums <= HIGH)
            return jnp.maximum(bad, jnp.max(jnp.where(fine, 0.0, 1.0), axis=0, keepdims=True))

        bad = lax.fori_loop(0, HEADS // 2, body, jnp.zeros((1, AUG), jnp.float32))
        flag_ref[0, 0] = jnp.max(bad)

    loads[1].wait()
    keys_values(tokens, 0, OWN)
    q_marks = jnp.concatenate([jnp.broadcast_to(query_marks(b), (BLK, AUG)) for b in range(4)], axis=0)
    project(OWN_KEYS, 0, q_marks.astype(jnp.bfloat16), 0, qa)

    def merge(slots, number):
        total = slots[0].astype(jnp.float32)
        for k in range(1, number):
            total = total + slots[k].astype(jnp.float32)
        return total.astype(jnp.bfloat16)

    halo_wait((0, 1, 2, 3))
    send_halo(both(up, left), halo.at[0], 9, {"col": col - 1})
    send_halo(both(up, right), halo.at[1], 8, {"col": col + 1})
    send_halo(both(down, left), halo.at[2], 11, {"col": col - 1})
    send_halo(both(down, right), halo.at[3], 10, {"col": col + 1})

    attend_own(0, 3)

    arrive1()
    mine[...] = merge(part1, n_row)
    start2()
    part2[col] = mine[...]

    attend_own(3, 6)

    for exists, _, arrives in cnt_copies:
        pl.when(exists)(lambda arrives=arrives: arrives.wait_recv())

    def halo_keys(begin):
        values = halo[begin : begin + 4].reshape(4 * BLK, WIDTH)
        keys_values(values, OWN_KEYS + begin * BLK, SLOTS[begin : begin + 4])

    halo_keys(0)

    arrive2()
    rtok[row] = merge(part2, n_col)
    start3()

    halo_wait((4, 5, 6, 7))
    halo_keys(4)
    halo_wait((8, 9, 10, 11))
    halo_keys(8)
    attend_halo()

    arrive3()
    saves = [
        pltpu.make_async_copy(halo, halo_out, save_sem.at[0]),
        pltpu.make_async_copy(rtok, rtok_out, save_sem.at[1]),
        pltpu.make_async_copy(cnts, cnts_out, save_sem.at[2]),
    ]
    for save in saves:
        save.start()
    keys_values(rtok[...].reshape(REGION, WIDTH), REGION_AT, None)
    attend_region()

    for cond, copy in sends:
        pl.when(cond)(lambda copy=copy: copy.wait_send())
    for exists, copy, _ in cnt_copies:
        pl.when(exists)(lambda copy=copy: copy.wait_send())
    leave1()
    leave2()
    leave3()
    for save in saves:
        save.wait()


def fused(n_row, n_col, tokens, gain, w_qkv, pattern, counts, region):
    chunk = REGION // n_row
    vmem = pl.BlockSpec(memory_space=pltpu.VMEM)
    smem = pl.BlockSpec(memory_space=pltpu.SMEM)
    anywhere = pl.BlockSpec(memory_space=pl.ANY)
    hbm = pl.BlockSpec(memory_space=pltpu.HBM)
    bf16, f32 = jnp.bfloat16, jnp.float32
    dma = pltpu.SemaphoreType.DMA
    flops = 2 * (OWN_KEYS * WIDTH * WIDTH * 3 + (KEYS - OWN_KEYS) * WIDTH * WIDTH * 2 + OWN_KEYS * 1408 * WIDTH * 2)
    return pl.pallas_call(
        functools.partial(kernel, n_row, n_col),
        out_shape=(
            pltpu.VMEM((OWN_KEYS, WIDTH), bf16),
            jax.ShapeDtypeStruct((1, 1), f32),
            jax.ShapeDtypeStruct((len(SLOTS), BLK, WIDTH), bf16),
            jax.ShapeDtypeStruct((n_row, chunk, WIDTH), bf16),
            jax.ShapeDtypeStruct((9, 8, 128), jnp.int32),
        ),
        in_specs=[hbm, hbm, hbm, smem, smem, hbm],
        out_specs=(vmem, smem, anywhere, anywhere, anywhere),
        scratch_shapes=[
            pltpu.VMEM((4, BLK, WIDTH), bf16),
            pltpu.VMEM((len(SLOTS), BLK, WIDTH), bf16),
            pltpu.VMEM((WIDTH, 3 * WIDTH), bf16),
            pltpu.VMEM((9, 8, 128), jnp.int32),
            pltpu.VMEM((n_row, chunk, WIDTH), bf16),
            pltpu.VMEM((n_row, chunk, WIDTH), bf16),
            pltpu.VMEM((chunk, WIDTH), bf16),
            pltpu.VMEM((n_col, chunk, WIDTH), bf16),
            pltpu.VMEM((n_row, chunk, WIDTH), bf16),
            pltpu.VMEM((OWN_KEYS, WIDTH), bf16),
            pltpu.VMEM((OWN_KEYS, HEADS * AUG), bf16),
            pltpu.VMEM((KEYS, HEADS * AUG), bf16),
            pltpu.VMEM((KEYS, HEADS * AUG), bf16),
            pltpu.VMEM((OWN_KEYS, HEADS * AUG), f32),
            pltpu.VMEM((WIDTH,), f32),
            pltpu.VMEM((REGION,), jnp.int32),
            dma((4,)),
            dma((12,)), dma((12,)),
            dma((9,)), dma((9,)),
            dma((n_row,)), dma((n_row,)),
            dma((n_col,)), dma((n_col,)),
            dma((n_row,)), dma((n_row,)),
            dma((3,)),
        ],
        compiler_params=pltpu.CompilerParams(
            collective_id=0, has_side_effects=True, vmem_limit_bytes=48 << 20
        ),
        cost_estimate=pl.CostEstimate(flops=flops, bytes_accessed=9 << 20, transcendentals=OWN_KEYS * 1408 * HEADS),
    )(tokens, gain, w_qkv, pattern, counts, region)


def stable(own, gain, w_qkv, pattern, row, col, n_row, n_col, halo, rtok, cnts):
    grid = {place: own[i] for i, place in enumerate(OWN)}
    grid.update({place: halo[i] for i, place in enumerate(SLOTS)})
    places = [(r, c) for r in range(4) for c in range(4)]
    rows = jnp.concatenate([grid[p] for p in places] + [rtok.reshape(REGION, WIDTH)], axis=0)
    qkv = dot(norm_rows(rows, gain), w_qkv).astype(jnp.bfloat16)
    valid = []
    for place in places:
        (tr, tc), (i, j) = tile_of(place)
        valid.append(jnp.arange(BLK) + (i * 2 + j) * BLK < cnts[3 * tr + tc, 0, 0])
    masks = []
    for block in range(4):
        i, j = divmod(block, 2)
        marks = []
        for number, (r, c) in enumerate(places):
            dr, dc = r - i, c - j
            if 0 <= dr < 3 and 0 <= dc < 3:
                a, b = row * 2 + r - 1, col * 2 + c - 1
                inside = (a >= 0) & (a < 2 * n_row) & (b >= 0) & (b < 2 * n_col)
                marks.append(valid[number] & inside & (pattern[block, 3 * dr + dc] > 0))
            else:
                marks.append(jnp.zeros((BLK,), bool))
        masks.append(jnp.concatenate(marks + [jnp.ones((REGION,), bool)]))
    mask = jnp.stack(masks)
    own_at = jnp.array([4 * r + c for r, c in OWN])
    query = qkv[: 16 * BLK, :WIDTH].reshape(16, BLK, HEADS, HDIM)[own_at]
    key = qkv[:, WIDTH : 2 * WIDTH].reshape(-1, HEADS, HDIM)
    value = qkv[:, 2 * WIDTH :].reshape(-1, HEADS, HDIM)

    def one_head(args):
        q, k, v = args
        scores = jnp.einsum("bqd,kd->bqk", q, k, preferred_element_type=jnp.float32) * (HDIM ** (-0.5))
        masked = jnp.where(mask[:, None, :], scores, -1e30)
        top = jnp.max(masked, axis=-1, keepdims=True)
        weights = jnp.where(mask[:, None, :], jnp.exp(masked - top), 0.0)
        probs = (weights / jnp.sum(weights, axis=-1, keepdims=True)).astype(jnp.bfloat16)
        return jnp.einsum("bqk,kd->bqd", probs, v, preferred_element_type=jnp.float32).astype(jnp.bfloat16)

    heads = lax.map(one_head, (query.transpose(2, 0, 1, 3), key.transpose(1, 0, 2), value.transpose(1, 0, 2)))
    joined = heads.transpose(1, 2, 0, 3).reshape(OWN_KEYS, WIDTH)
    return with_layout_constraint(joined, Layout(major_to_minor=(0, 1)))


def local(n_row, n_col, tokens, gain, w_qkv, pattern, counts, region):
    own = tokens.reshape(4, BLK, WIDTH)
    blocks = pattern.reshape(4, 9)
    out, flag, halo, rtok, cnts = fused(
        n_row, n_col, own, gain, w_qkv, blocks, counts, region
    )
    row, col = lax.axis_index("row"), lax.axis_index("col")
    result = lax.cond(
        flag[0, 0] > 0.0,
        lambda: stable(own, gain.reshape(1, WIDTH), w_qkv, blocks, row, col, n_row, n_col, halo, rtok, cnts),
        lambda: out,
    )
    live = jnp.arange(OWN_KEYS, dtype=jnp.int32) < counts[0, 0]
    return jnp.where(live[:, None], result, jnp.zeros_like(result)).reshape(tokens.shape)


def solution(mesh):
    in_specs = (
        P(("scan", "row"), "col", None, None, None, None),
        P(),
        P(),
        P(("scan", "row"), "col", None, None, None),
        P(("scan", "row"), "col"),
        P("scan"),
    )
    out_specs = P(("scan", "row"), "col", None, None, None, None)
    body = functools.partial(local, mesh.shape["row"], mesh.shape["col"])
    return jax.shard_map(body, mesh=mesh, in_specs=in_specs, out_specs=out_specs, check_vma=False)
```

```python
import functools

import jax
import jax.numpy as jnp
from jax import lax
from jax.experimental import pallas as pl
from jax.experimental.layout import Layout, with_layout_constraint
from jax.experimental.pallas import tpu as pltpu
from jax.sharding import PartitionSpec as P

HEADS = 12
HDIM = 64
BLK = 128
WIDTH = HEADS * HDIM
AUG = 2 * HDIM
REGION = 256
MESH = pl.DeviceIdType.MESH
EXP_SCALE = (HDIM ** (-0.5)) * 1.4426950408889634
FAR = -1e30
LOW, HIGH = 2.0 ** (-80), 2.0**100

SLOTS = ((0, 1), (0, 2), (3, 1), (3, 2), (1, 0), (2, 0), (1, 3), (2, 3), (0, 0), (0, 3), (3, 0), (3, 3))
OWN = ((1, 1), (1, 2), (2, 1), (2, 2))
OWN_KEYS = 4 * BLK
HALO_KEYS = len(SLOTS) * BLK
REGION_AT = OWN_KEYS + HALO_KEYS
KEYS = REGION_AT + REGION


def dot(a, b):
    return lax.dot_general(a, b, (((1,), (0,)), ((), ())), preferred_element_type=jnp.float32)


def dot_t(a, b):
    return lax.dot_general(a, b, (((1,), (1,)), ((), ())), preferred_element_type=jnp.float32)


def norm_rows(values, gain):
    floats = values.astype(jnp.float32)
    center = floats - jnp.sum(floats, axis=-1, keepdims=True) * (1.0 / WIDTH)
    spread = jnp.sum(center * center, axis=-1, keepdims=True) * (1.0 / WIDTH)
    return (center * lax.rsqrt(spread + 1e-05) * gain).astype(jnp.bfloat16)


def tile_of(place):
    return tuple((0, 1, 1, 2)[p] for p in place), tuple((1, 0, 1, 0)[p] for p in place)


def kernel(
    n_row, n_col,
    tok_hbm, gain_hbm, w_hbm, pat_ref, cnt_ref, reg_hbm,
    out_ref, flag_ref, halo_out, rtok_out, cnts_out,
    own, halo, weights, cnts, picks, part1, mine, part2, rtok, normed, qa, ka, va, oa, gain_ref, reg_ref,
    load_sem, halo_send, halo_recv, cnt_send, cnt_recv, p1_send, p1_recv, p2_send, p2_recv, p3_send, p3_recv, save_sem,
):
    row, col = lax.axis_index("row"), lax.axis_index("col")
    up, down, left, right = row > 0, row < n_row - 1, col > 0, col < n_col - 1
    exists_r, exists_c = (up, None, None, down), (left, None, None, right)
    chunk = REGION // n_row

    def both(a, b):
        return b if a is None else (a if b is None else a & b)

    def there(place):
        return both(exists_r[place[0]], exists_c[place[1]])

    loads = [
        pltpu.make_async_copy(tok_hbm, own, load_sem.at[0]),
        pltpu.make_async_copy(w_hbm, weights, load_sem.at[1]),
        pltpu.make_async_copy(gain_hbm, gain_ref, load_sem.at[2]),
        pltpu.make_async_copy(reg_hbm, reg_ref, load_sem.at[3]),
    ]
    for load in loads:
        load.start()

    barrier = pltpu.get_barrier_semaphore()
    diagonals = [(dr, dc) for dr in (-1, 1) for dc in (-1, 1)]

    def signal_row(r, _):
        @pl.when(r != row)
        def _():
            pl.semaphore_signal(barrier, inc=1, device_id={"row": r}, device_id_type=MESH)
        return 0

    def signal_col(c, _):
        @pl.when(c != col)
        def _():
            pl.semaphore_signal(barrier, inc=1, device_id={"col": c}, device_id_type=MESH)
        return 0

    lax.fori_loop(0, n_row, signal_row, 0)
    lax.fori_loop(0, n_col, signal_col, 0)
    for dr, dc in diagonals:
        @pl.when(both(up if dr < 0 else down, left if dc < 0 else right))
        def _(dr=dr, dc=dc):
            pl.semaphore_signal(barrier, inc=1, device_id={"row": row + dr, "col": col + dc}, device_id_type=MESH)

    as_int = lambda flag: jnp.where(flag, 1, 0)
    n_diag = (as_int(up) + as_int(down)) * (as_int(left) + as_int(right))

    for group in range(4):
        @pl.when(jnp.logical_not((up, down, left, right)[group]))
        def _(group=group):
            halo[2 * group : 2 * group + 2] = jnp.zeros((2, BLK, WIDTH), jnp.bfloat16)
    for slot in range(8, 12):
        @pl.when(jnp.logical_not(there(SLOTS[slot])))
        def _(slot=slot):
            halo[slot] = jnp.zeros((BLK, WIDTH), jnp.bfloat16)
    count = cnt_ref[0, 0]
    for t in range(9):
        if t == 4:
            cnts[t] = jnp.broadcast_to(count, (8, 128)).astype(jnp.int32)
        else:
            dr, dc = t // 3 - 1, t % 3 - 1
            exists = both((up, None, down)[dr + 1], (left, None, right)[dc + 1])

            @pl.when(jnp.logical_not(exists))
            def _(t=t):
                cnts[t] = jnp.zeros((8, 128), jnp.int32)

    loads[0].wait()
    loads[2].wait()
    loads[3].wait()

    tokens = own[...].reshape(OWN_KEYS, WIDTH)
    first = (row * n_col + col) * OWN_KEYS
    flat = lax.broadcasted_iota(jnp.int32, (OWN_KEYS, REGION), 0) + first
    hit = jnp.where(flat == reg_ref[...][None, :], 1.0, 0.0).astype(jnp.bfloat16)
    found = lax.dot_general(hit, tokens, (((0,), (0,)), ((), ())), preferred_element_type=jnp.float32)
    picks[...] = found.astype(jnp.bfloat16).reshape(n_row, chunk, WIDTH)

    pl.semaphore_wait(barrier, n_row + n_col - 2 + n_diag)

    def remote(src, dst, send, recv, device):
        return pltpu.make_async_remote_copy(
            src_ref=src, dst_ref=dst, send_sem=send, recv_sem=recv, device_id=device, device_id_type=MESH
        )

    sends = []

    def send_halo(cond, src, slot, device):
        copy = remote(src, halo.at[slot], halo_send.at[len(sends)], halo_recv.at[slot], device)
        sends.append((cond, copy))
        pl.when(cond)(lambda: copy.start())

    def halo_wait(slots):
        for slot in slots:
            copy = remote(halo.at[slot], halo.at[slot], halo_send.at[slot], halo_recv.at[slot], {"row": row})
            pl.when(there(SLOTS[slot]))(lambda copy=copy: copy.wait_recv())

    cnt_copies = []
    for t in range(9):
        if t != 4:
            dr, dc = t // 3 - 1, t % 3 - 1
            exists = both((up, None, down)[dr + 1], (left, None, right)[dc + 1])
            device = {}
            if dr:
                device["row"] = row + dr
            if dc:
                device["col"] = col + dc
            copy = remote(cnts.at[4], cnts.at[8 - t], cnt_send.at[t], cnt_recv.at[8 - t], device)
            arrives = remote(cnts.at[4], cnts.at[t], cnt_send.at[t], cnt_recv.at[t], device)
            cnt_copies.append((exists, copy, arrives))
            pl.when(exists)(lambda copy=copy: copy.start())

    def exchange(size, axis, me, source, target, send_sem, recv_sem):
        def copy_to(k):
            return remote(source(k), target(me), send_sem.at[k], recv_sem.at[me], {axis: k})

        def copy_from(k):
            return remote(source(k), target(k), send_sem.at[k], recv_sem.at[k], {axis: k})

        def start(k, _):
            pl.when(k != me)(lambda: copy_to(k).start())
            return 0

        def arrive(k, _):
            pl.when(k != me)(lambda: copy_from(k).wait_recv())
            return 0

        def leave(k, _):
            pl.when(k != me)(lambda: copy_to(k).wait_send())
            return 0

        return tuple(lambda body=body: lax.fori_loop(0, size, body, 0) for body in (start, arrive, leave))

    start1, arrive1, leave1 = exchange(
        n_row, "row", row, lambda k: picks.at[k], lambda k: part1.at[k], p1_send, p1_recv
    )
    start2, arrive2, leave2 = exchange(n_col, "col", col, lambda k: mine, lambda k: part2.at[k], p2_send, p2_recv)
    start3, arrive3, leave3 = exchange(
        n_row, "row", row, lambda k: rtok.at[row], lambda k: rtok.at[k], p3_send, p3_recv
    )
    send_halo(up, own.at[0], 2, {"row": row - 1})
    send_halo(up, own.at[1], 3, {"row": row - 1})
    send_halo(down, own.at[2], 0, {"row": row + 1})
    send_halo(down, own.at[3], 1, {"row": row + 1})

    start1()
    part1[row] = picks[row]

    send_halo(left, own.at[0], 6, {"col": col - 1})
    send_halo(left, own.at[2], 7, {"col": col - 1})
    send_halo(right, own.at[1], 4, {"col": col + 1})
    send_halo(right, own.at[3], 5, {"col": col + 1})

    lane = lax.broadcasted_iota(jnp.int32, (1, AUG), 1)
    spare = lax.rem(lane, HDIM)
    low_half = lane < HDIM

    def query_marks(block):
        i, j = divmod(block, 2)
        marks = jnp.where(spare <= 16, FAR, 0.0)
        for k in range(9):
            place = (i + k // 3, j + k % 3)
            allowed = pat_ref[block, k].astype(jnp.float32)
            exists = there(place)
            if exists is not None:
                allowed = allowed * as_int(exists).astype(jnp.float32)
            marks = jnp.where(spare == place[0] * 4 + place[1], (1.0 - allowed) * FAR, marks)
        return marks

    def key_marks(place):
        (tr, tc), (i, j) = tile_of(place)
        position = lax.broadcasted_iota(jnp.int32, (BLK, AUG), 0) + (i * 2 + j) * BLK
        beyond = jnp.where(position >= cnts[3 * tr + tc, 0:1, :], 1.0, 0.0)
        return jnp.where(spare == 16, beyond, jnp.where(spare == place[0] * 4 + place[1], 1.0, 0.0))

    def halves(pair, other):
        return jnp.where(low_half, pair, other), jnp.where(low_half, other, pair)

    def project(n, key_at, marks, part, out):
        for j in range(3):
            at = part * WIDTH + j * 256
            result = dot(normed[0:n, :], weights[:, at : at + 256]).astype(jnp.bfloat16)
            for t in range(2):
                pair = result[:, t * 128 : t * 128 + 128]
                to = j * 512 + t * 256
                first_head, second_head = halves(pair, marks)
                out[key_at : key_at + n, to : to + 128] = first_head
                out[key_at : key_at + n, to + 128 : to + 256] = second_head

    def keys_values(values, key_at, places):
        n = values.shape[0]
        normed[0:n, :] = norm_rows(values, gain_ref[...][None, :])
        if places is None:
            marks = jnp.zeros((n, AUG), jnp.bfloat16)
        else:
            marks = jnp.concatenate([key_marks(place) for place in places], axis=0).astype(jnp.bfloat16)
        project(n, key_at, marks, 1, ka)
        project(n, key_at, jnp.ones((n, AUG), jnp.bfloat16), 2, va)

    def lanes(pair, half):
        return pl.ds(pl.multiple_of(pair * (2 * AUG) + half * AUG, AUG), AUG)

    def part_of(blocks, keys, at):
        def stacked(ref, groups):
            return jnp.concatenate([ref[begin : begin + n, at] for begin, n in groups], axis=0)

        scores = dot_t(stacked(qa, [(b * BLK, BLK) for b in blocks]), stacked(ka, keys))
        probs = jnp.exp2(scores * EXP_SCALE).astype(jnp.bfloat16)
        return dot(probs, stacked(va, keys))

    def attend_own(begin, end):
        def body(pair, _):
            for half in range(2):
                at = lanes(pair, half)
                oa[:, at] = part_of(range(4), ((0, OWN_KEYS),), at)
            return 0

        lax.fori_loop(begin, end, body, 0)

    def slots_at(*groups):
        return tuple((OWN_KEYS + slot * BLK, n * BLK) for slot, n in groups)

    def attend_beside():
        def body(pair, _):
            for half in range(2):
                at = lanes(pair, half)
                sides = (part_of((0, 2), slots_at((4, 2)), at), part_of((1, 3), slots_at((6, 2)), at))
                for b in range(4):
                    i, j = divmod(b, 2)
                    oa[b * BLK : b * BLK + BLK, at] += sides[j][i * BLK : i * BLK + BLK]
            return 0

        lax.fori_loop(0, HEADS // 2, body, 0)

    def attend_across():
        def body(pair, _):
            for half in range(2):
                at = lanes(pair, half)
                above = part_of((0, 1), slots_at((0, 2), (8, 2)), at)
                below = part_of((2, 3), slots_at((2, 2), (10, 2)), at)
                oa[0 : 2 * BLK, at] += above
                oa[2 * BLK : 4 * BLK, at] += below
            return 0

        lax.fori_loop(0, HEADS // 2, body, 0)

    def attend_region():
        def body(pair, bad):
            one, two = (
                oa[:, lanes(pair, half)] + part_of(range(4), ((REGION_AT, REGION),), lanes(pair, half))
                for half in range(2)
            )
            sums = pltpu.roll(jnp.where(low_half, two, one), HDIM, 1)
            result = jnp.where(low_half, one, two) / sums
            out_ref[:, pl.ds(pl.multiple_of(pair * AUG, AUG), AUG)] = result.astype(jnp.bfloat16)
            fine = (sums >= LOW) & (sums <= HIGH)
            return jnp.maximum(bad, jnp.max(jnp.where(fine, 0.0, 1.0), axis=0, keepdims=True))

        bad = lax.fori_loop(0, HEADS // 2, body, jnp.zeros((1, AUG), jnp.float32))
        flag_ref[0, 0] = jnp.max(bad)

    loads[1].wait()
    keys_values(tokens, 0, OWN)
    q_marks = jnp.concatenate([jnp.broadcast_to(query_marks(b), (BLK, AUG)) for b in range(4)], axis=0)
    project(OWN_KEYS, 0, q_marks.astype(jnp.bfloat16), 0, qa)

    def merge(slots, number):
        total = slots[0].astype(jnp.float32)
        for k in range(1, number):
            total = total + slots[k].astype(jnp.float32)
        return total.astype(jnp.bfloat16)

    attend_own(0, 3)

    halo_wait((0, 1, 2, 3, 4, 5, 6, 7))
    send_halo(both(up, right), halo.at[1], 8, {"col": col + 1})
    send_halo(both(down, left), halo.at[2], 11, {"col": col - 1})
    send_halo(both(right, down), halo.at[7], 9, {"row": row + 1})
    send_halo(both(left, up), halo.at[4], 10, {"row": row - 1})

    arrive1()
    mine[...] = merge(part1, n_row)
    start2()
    part2[col] = mine[...]

    attend_own(3, 6)

    for exists, _, arrives in cnt_copies:
        pl.when(exists)(lambda arrives=arrives: arrives.wait_recv())

    def halo_keys(begin):
        values = halo[begin : begin + 4].reshape(4 * BLK, WIDTH)
        keys_values(values, OWN_KEYS + begin * BLK, SLOTS[begin : begin + 4])

    halo_keys(0)
    halo_keys(4)

    arrive2()
    rtok[row] = merge(part2, n_col)
    start3()

    attend_beside()
    halo_wait((8, 9, 10, 11))
    halo_keys(8)
    attend_across()

    arrive3()
    saves = [
        pltpu.make_async_copy(halo, halo_out, save_sem.at[0]),
        pltpu.make_async_copy(rtok, rtok_out, save_sem.at[1]),
        pltpu.make_async_copy(cnts, cnts_out, save_sem.at[2]),
    ]
    for save in saves:
        save.start()
    keys_values(rtok[...].reshape(REGION, WIDTH), REGION_AT, None)
    attend_region()

    for cond, copy in sends:
        pl.when(cond)(lambda copy=copy: copy.wait_send())
    for exists, copy, _ in cnt_copies:
        pl.when(exists)(lambda copy=copy: copy.wait_send())
    leave1()
    leave2()
    leave3()
    for save in saves:
        save.wait()


def fused(n_row, n_col, tokens, gain, w_qkv, pattern, counts, region):
    chunk = REGION // n_row
    vmem = pl.BlockSpec(memory_space=pltpu.VMEM)
    smem = pl.BlockSpec(memory_space=pltpu.SMEM)
    anywhere = pl.BlockSpec(memory_space=pl.ANY)
    hbm = pl.BlockSpec(memory_space=pltpu.HBM)
    bf16, f32 = jnp.bfloat16, jnp.float32
    dma = pltpu.SemaphoreType.DMA
    flops = 2 * (OWN_KEYS * WIDTH * WIDTH * 3 + (KEYS - OWN_KEYS) * WIDTH * WIDTH * 2 + OWN_KEYS * 1408 * WIDTH * 2)
    return pl.pallas_call(
        functools.partial(kernel, n_row, n_col),
        out_shape=(
            pltpu.VMEM((OWN_KEYS, WIDTH), bf16),
            jax.ShapeDtypeStruct((1, 1), f32),
            jax.ShapeDtypeStruct((len(SLOTS), BLK, WIDTH), bf16),
            jax.ShapeDtypeStruct((n_row, chunk, WIDTH), bf16),
            jax.ShapeDtypeStruct((9, 8, 128), jnp.int32),
        ),
        in_specs=[hbm, hbm, hbm, smem, smem, hbm],
        out_specs=(vmem, smem, anywhere, anywhere, anywhere),
        scratch_shapes=[
            pltpu.VMEM((4, BLK, WIDTH), bf16),
            pltpu.VMEM((len(SLOTS), BLK, WIDTH), bf16),
            pltpu.VMEM((WIDTH, 3 * WIDTH), bf16),
            pltpu.VMEM((9, 8, 128), jnp.int32),
            pltpu.VMEM((n_row, chunk, WIDTH), bf16),
            pltpu.VMEM((n_row, chunk, WIDTH), bf16),
            pltpu.VMEM((chunk, WIDTH), bf16),
            pltpu.VMEM((n_col, chunk, WIDTH), bf16),
            pltpu.VMEM((n_row, chunk, WIDTH), bf16),
            pltpu.VMEM((OWN_KEYS, WIDTH), bf16),
            pltpu.VMEM((OWN_KEYS, HEADS * AUG), bf16),
            pltpu.VMEM((KEYS, HEADS * AUG), bf16),
            pltpu.VMEM((KEYS, HEADS * AUG), bf16),
            pltpu.VMEM((OWN_KEYS, HEADS * AUG), f32),
            pltpu.VMEM((WIDTH,), f32),
            pltpu.VMEM((REGION,), jnp.int32),
            dma((4,)),
            dma((12,)), dma((12,)),
            dma((9,)), dma((9,)),
            dma((n_row,)), dma((n_row,)),
            dma((n_col,)), dma((n_col,)),
            dma((n_row,)), dma((n_row,)),
            dma((3,)),
        ],
        compiler_params=pltpu.CompilerParams(
            collective_id=0, has_side_effects=True, vmem_limit_bytes=48 << 20
        ),
        cost_estimate=pl.CostEstimate(flops=flops, bytes_accessed=9 << 20, transcendentals=OWN_KEYS * 1408 * HEADS),
    )(tokens, gain, w_qkv, pattern, counts, region)


def stable(own, gain, w_qkv, pattern, row, col, n_row, n_col, halo, rtok, cnts):
    grid = {place: own[i] for i, place in enumerate(OWN)}
    grid.update({place: halo[i] for i, place in enumerate(SLOTS)})
    places = [(r, c) for r in range(4) for c in range(4)]
    rows = jnp.concatenate([grid[p] for p in places] + [rtok.reshape(REGION, WIDTH)], axis=0)
    qkv = dot(norm_rows(rows, gain), w_qkv).astype(jnp.bfloat16)
    valid = []
    for place in places:
        (tr, tc), (i, j) = tile_of(place)
        valid.append(jnp.arange(BLK) + (i * 2 + j) * BLK < cnts[3 * tr + tc, 0, 0])
    masks = []
    for block in range(4):
        i, j = divmod(block, 2)
        marks = []
        for number, (r, c) in enumerate(places):
            dr, dc = r - i, c - j
            if 0 <= dr < 3 and 0 <= dc < 3:
                a, b = row * 2 + r - 1, col * 2 + c - 1
                inside = (a >= 0) & (a < 2 * n_row) & (b >= 0) & (b < 2 * n_col)
                marks.append(valid[number] & inside & (pattern[block, 3 * dr + dc] > 0))
            else:
                marks.append(jnp.zeros((BLK,), bool))
        masks.append(jnp.concatenate(marks + [jnp.ones((REGION,), bool)]))
    mask = jnp.stack(masks)
    own_at = jnp.array([4 * r + c for r, c in OWN])
    query = qkv[: 16 * BLK, :WIDTH].reshape(16, BLK, HEADS, HDIM)[own_at]
    key = qkv[:, WIDTH : 2 * WIDTH].reshape(-1, HEADS, HDIM)
    value = qkv[:, 2 * WIDTH :].reshape(-1, HEADS, HDIM)

    def one_head(args):
        q, k, v = args
        scores = jnp.einsum("bqd,kd->bqk", q, k, preferred_element_type=jnp.float32) * (HDIM ** (-0.5))
        masked = jnp.where(mask[:, None, :], scores, -1e30)
        top = jnp.max(masked, axis=-1, keepdims=True)
        weights = jnp.where(mask[:, None, :], jnp.exp(masked - top), 0.0)
        probs = (weights / jnp.sum(weights, axis=-1, keepdims=True)).astype(jnp.bfloat16)
        return jnp.einsum("bqk,kd->bqd", probs, v, preferred_element_type=jnp.float32).astype(jnp.bfloat16)

    heads = lax.map(one_head, (query.transpose(2, 0, 1, 3), key.transpose(1, 0, 2), value.transpose(1, 0, 2)))
    joined = heads.transpose(1, 2, 0, 3).reshape(OWN_KEYS, WIDTH)
    return with_layout_constraint(joined, Layout(major_to_minor=(0, 1)))


def local(n_row, n_col, tokens, gain, w_qkv, pattern, counts, region):
    own = tokens.reshape(4, BLK, WIDTH)
    blocks = pattern.reshape(4, 9)
    out, flag, halo, rtok, cnts = fused(
        n_row, n_col, own, gain, w_qkv, blocks, counts, region
    )
    row, col = lax.axis_index("row"), lax.axis_index("col")
    result = lax.cond(
        flag[0, 0] > 0.0,
        lambda: stable(own, gain.reshape(1, WIDTH), w_qkv, blocks, row, col, n_row, n_col, halo, rtok, cnts),
        lambda: out,
    )
    live = jnp.arange(OWN_KEYS, dtype=jnp.int32) < counts[0, 0]
    return jnp.where(live[:, None], result, jnp.zeros_like(result)).reshape(tokens.shape)


def solution(mesh):
    in_specs = (
        P(("scan", "row"), "col", None, None, None, None),
        P(),
        P(),
        P(("scan", "row"), "col", None, None, None),
        P(("scan", "row"), "col"),
        P("scan"),
    )
    out_specs = P(("scan", "row"), "col", None, None, None, None)
    body = functools.partial(local, mesh.shape["row"], mesh.shape["col"])
    return jax.shard_map(body, mesh=mesh, in_specs=in_specs, out_specs=out_specs, check_vma=False)
```

```python
import functools

import jax
import jax.numpy as jnp
from jax import lax
from jax.experimental import pallas as pl
from jax.experimental.layout import Layout, with_layout_constraint
from jax.experimental.pallas import tpu as pltpu
from jax.sharding import PartitionSpec as P

HEADS = 12
HDIM = 64
BLK = 128
WIDTH = HEADS * HDIM
AUG = 2 * HDIM
REGION = 256
MESH = pl.DeviceIdType.MESH
EXP_SCALE = (HDIM ** (-0.5)) * 1.4426950408889634
FAR = -1e30
LOW, HIGH = 2.0 ** (-80), 2.0**100

SLOTS = ((0, 1), (0, 2), (3, 1), (3, 2), (1, 0), (2, 0), (1, 3), (2, 3), (0, 0), (0, 3), (3, 0), (3, 3))
OWN = ((1, 1), (1, 2), (2, 1), (2, 2))
OWN_KEYS = 4 * BLK
HALO_KEYS = len(SLOTS) * BLK
REGION_AT = OWN_KEYS + HALO_KEYS
KEYS = REGION_AT + REGION


def dot(a, b):
    return lax.dot_general(a, b, (((1,), (0,)), ((), ())), preferred_element_type=jnp.float32)


def dot_t(a, b):
    return lax.dot_general(a, b, (((1,), (1,)), ((), ())), preferred_element_type=jnp.float32)


def norm_rows(values, gain):
    floats = values.astype(jnp.float32)
    center = floats - jnp.sum(floats, axis=-1, keepdims=True) * (1.0 / WIDTH)
    spread = jnp.sum(center * center, axis=-1, keepdims=True) * (1.0 / WIDTH)
    return (center * lax.rsqrt(spread + 1e-05) * gain).astype(jnp.bfloat16)


def tile_of(place):
    return tuple((0, 1, 1, 2)[p] for p in place), tuple((1, 0, 1, 0)[p] for p in place)


def kernel(
    n_row, n_col,
    tok_hbm, gain_hbm, w_hbm, pat_ref, cnt_ref, reg_hbm,
    out_ref, flag_ref, halo_out, rtok_out, cnts_out,
    own, halo, weights, cnts, picks, part1, mine, part2, rtok, normed, qa, ka, va, oa, gain_ref, reg_ref,
    load_sem, halo_send, halo_recv, cnt_send, cnt_recv, p1_send, p1_recv, p2_send, p2_recv, p3_send, p3_recv, save_sem,
):
    row, col = lax.axis_index("row"), lax.axis_index("col")
    up, down, left, right = row > 0, row < n_row - 1, col > 0, col < n_col - 1
    exists_r, exists_c = (up, None, None, down), (left, None, None, right)
    chunk = REGION // n_row

    def both(a, b):
        return b if a is None else (a if b is None else a & b)

    def there(place):
        return both(exists_r[place[0]], exists_c[place[1]])

    loads = [
        pltpu.make_async_copy(tok_hbm, own, load_sem.at[0]),
        pltpu.make_async_copy(w_hbm, weights, load_sem.at[1]),
        pltpu.make_async_copy(gain_hbm, gain_ref, load_sem.at[2]),
        pltpu.make_async_copy(reg_hbm, reg_ref, load_sem.at[3]),
    ]
    for load in loads:
        load.start()

    barrier = pltpu.get_barrier_semaphore()
    diagonals = [(dr, dc) for dr in (-1, 1) for dc in (-1, 1)]

    def signal_row(r, _):
        @pl.when(r != row)
        def _():
            pl.semaphore_signal(barrier, inc=1, device_id={"row": r}, device_id_type=MESH)
        return 0

    def signal_col(c, _):
        @pl.when(c != col)
        def _():
            pl.semaphore_signal(barrier, inc=1, device_id={"col": c}, device_id_type=MESH)
        return 0

    lax.fori_loop(0, n_row, signal_row, 0)
    lax.fori_loop(0, n_col, signal_col, 0)
    for dr, dc in diagonals:
        @pl.when(both(up if dr < 0 else down, left if dc < 0 else right))
        def _(dr=dr, dc=dc):
            pl.semaphore_signal(barrier, inc=1, device_id={"row": row + dr, "col": col + dc}, device_id_type=MESH)

    as_int = lambda flag: jnp.where(flag, 1, 0)
    n_diag = (as_int(up) + as_int(down)) * (as_int(left) + as_int(right))

    for group in range(4):
        @pl.when(jnp.logical_not((up, down, left, right)[group]))
        def _(group=group):
            halo[2 * group : 2 * group + 2] = jnp.zeros((2, BLK, WIDTH), jnp.bfloat16)
    for slot in range(8, 12):
        @pl.when(jnp.logical_not(there(SLOTS[slot])))
        def _(slot=slot):
            halo[slot] = jnp.zeros((BLK, WIDTH), jnp.bfloat16)
    count = cnt_ref[0, 0]
    for t in range(9):
        if t == 4:
            cnts[t] = jnp.broadcast_to(count, (8, 128)).astype(jnp.int32)
        else:
            dr, dc = t // 3 - 1, t % 3 - 1
            exists = both((up, None, down)[dr + 1], (left, None, right)[dc + 1])

            @pl.when(jnp.logical_not(exists))
            def _(t=t):
                cnts[t] = jnp.zeros((8, 128), jnp.int32)

    loads[0].wait()
    loads[2].wait()
    loads[3].wait()

    tokens = own[...].reshape(OWN_KEYS, WIDTH)
    first = (row * n_col + col) * OWN_KEYS
    flat = lax.broadcasted_iota(jnp.int32, (OWN_KEYS, REGION), 0) + first
    hit = jnp.where(flat == reg_ref[...][None, :], 1.0, 0.0).astype(jnp.bfloat16)
    found = lax.dot_general(hit, tokens, (((0,), (0,)), ((), ())), preferred_element_type=jnp.float32)
    picks[...] = found.astype(jnp.bfloat16).reshape(n_row, chunk, WIDTH)

    pl.semaphore_wait(barrier, n_row + n_col - 2 + n_diag)

    def remote(src, dst, send, recv, device):
        return pltpu.make_async_remote_copy(
            src_ref=src, dst_ref=dst, send_sem=send, recv_sem=recv, device_id=device, device_id_type=MESH
        )

    sends = []

    def send_halo(cond, src, slot, device):
        copy = remote(src, halo.at[slot], halo_send.at[len(sends)], halo_recv.at[slot], device)
        sends.append((cond, copy))
        pl.when(cond)(lambda: copy.start())

    def halo_wait(slots):
        for slot in slots:
            copy = remote(halo.at[slot], halo.at[slot], halo_send.at[slot], halo_recv.at[slot], {"row": row})
            pl.when(there(SLOTS[slot]))(lambda copy=copy: copy.wait_recv())

    cnt_copies = []
    for t in range(9):
        if t != 4:
            dr, dc = t // 3 - 1, t % 3 - 1
            exists = both((up, None, down)[dr + 1], (left, None, right)[dc + 1])
            device = {}
            if dr:
                device["row"] = row + dr
            if dc:
                device["col"] = col + dc
            copy = remote(cnts.at[4], cnts.at[8 - t], cnt_send.at[t], cnt_recv.at[8 - t], device)
            arrives = remote(cnts.at[4], cnts.at[t], cnt_send.at[t], cnt_recv.at[t], device)
            cnt_copies.append((exists, copy, arrives))
            pl.when(exists)(lambda copy=copy: copy.start())

    def exchange(size, axis, me, source, target, send_sem, recv_sem):
        def copy_to(k):
            return remote(source(k), target(me), send_sem.at[k], recv_sem.at[me], {axis: k})

        def copy_from(k):
            return remote(source(k), target(k), send_sem.at[k], recv_sem.at[k], {axis: k})

        def start(k, _):
            pl.when(k != me)(lambda: copy_to(k).start())
            return 0

        def arrive(k, _):
            pl.when(k != me)(lambda: copy_from(k).wait_recv())
            return 0

        def leave(k, _):
            pl.when(k != me)(lambda: copy_to(k).wait_send())
            return 0

        return tuple(lambda body=body: lax.fori_loop(0, size, body, 0) for body in (start, arrive, leave))

    start1, arrive1, leave1 = exchange(
        n_row, "row", row, lambda k: picks.at[k], lambda k: part1.at[k], p1_send, p1_recv
    )
    start2, arrive2, leave2 = exchange(n_col, "col", col, lambda k: mine, lambda k: part2.at[k], p2_send, p2_recv)
    start3, arrive3, leave3 = exchange(
        n_row, "row", row, lambda k: rtok.at[row], lambda k: rtok.at[k], p3_send, p3_recv
    )
    send_halo(up, own.at[0], 2, {"row": row - 1})
    send_halo(up, own.at[1], 3, {"row": row - 1})
    send_halo(down, own.at[2], 0, {"row": row + 1})
    send_halo(down, own.at[3], 1, {"row": row + 1})

    start1()
    part1[row] = picks[row]

    send_halo(left, own.at[0], 6, {"col": col - 1})
    send_halo(left, own.at[2], 7, {"col": col - 1})
    send_halo(right, own.at[1], 4, {"col": col + 1})
    send_halo(right, own.at[3], 5, {"col": col + 1})

    lane = lax.broadcasted_iota(jnp.int32, (1, AUG), 1)
    spare = lax.rem(lane, HDIM)
    low_half = lane < HDIM

    def query_marks(block):
        i, j = divmod(block, 2)
        marks = jnp.where(spare <= 16, FAR, 0.0)
        for k in range(9):
            place = (i + k // 3, j + k % 3)
            allowed = pat_ref[block, k].astype(jnp.float32)
            exists = there(place)
            if exists is not None:
                allowed = allowed * as_int(exists).astype(jnp.float32)
            marks = jnp.where(spare == place[0] * 4 + place[1], (1.0 - allowed) * FAR, marks)
        return marks

    def key_marks(place):
        (tr, tc), (i, j) = tile_of(place)
        position = lax.broadcasted_iota(jnp.int32, (BLK, AUG), 0) + (i * 2 + j) * BLK
        beyond = jnp.where(position >= cnts[3 * tr + tc, 0:1, :], 1.0, 0.0)
        return jnp.where(spare == 16, beyond, jnp.where(spare == place[0] * 4 + place[1], 1.0, 0.0))

    def halves(pair, other):
        return jnp.where(low_half, pair, other), jnp.where(low_half, other, pair)

    def project(n, key_at, marks, part, out):
        for j in range(3):
            at = part * WIDTH + j * 256
            result = dot(normed[0:n, :], weights[:, at : at + 256]).astype(jnp.bfloat16)
            for t in range(2):
                pair = result[:, t * 128 : t * 128 + 128]
                to = j * 512 + t * 256
                first_head, second_head = halves(pair, marks)
                out[key_at : key_at + n, to : to + 128] = first_head
                out[key_at : key_at + n, to + 128 : to + 256] = second_head

    def keys_values(values, key_at, places):
        n = values.shape[0]
        normed[0:n, :] = norm_rows(values, gain_ref[...][None, :])
        if places is None:
            marks = jnp.zeros((n, AUG), jnp.bfloat16)
        else:
            marks = jnp.concatenate([key_marks(place) for place in places], axis=0).astype(jnp.bfloat16)
        project(n, key_at, marks, 1, ka)
        project(n, key_at, jnp.ones((n, AUG), jnp.bfloat16), 2, va)

    def lanes(pair, half):
        return pl.ds(pl.multiple_of(pair * (2 * AUG) + half * AUG, AUG), AUG)

    def part_of(blocks, keys, at):
        def stacked(ref, groups):
            return jnp.concatenate([ref[begin : begin + n, at] for begin, n in groups], axis=0)

        scores = dot_t(stacked(qa, [(b * BLK, BLK) for b in blocks]), stacked(ka, keys))
        probs = jnp.exp2(scores * EXP_SCALE).astype(jnp.bfloat16)
        return dot(probs, stacked(va, keys))

    def attend_own(begin, end):
        def body(pair, _):
            for half in range(2):
                at = lanes(pair, half)
                oa[:, at] = part_of(range(4), ((0, OWN_KEYS),), at)
            return 0

        lax.fori_loop(begin, end, body, 0)

    def slots_at(*groups):
        return tuple((OWN_KEYS + slot * BLK, n * BLK) for slot, n in groups)

    def attend_beside():
        def body(four, _):
            for head in range(4):
                at = lanes(four * 2 + head // 2, head % 2)
                sides = (part_of((0, 2), slots_at((4, 2)), at), part_of((1, 3), slots_at((6, 2)), at))
                for b in range(4):
                    i, j = divmod(b, 2)
                    oa[b * BLK : b * BLK + BLK, at] += sides[j][i * BLK : i * BLK + BLK]
            return 0

        lax.fori_loop(0, HEADS // 4, body, 0)

    def attend_across():
        def body(four, _):
            for head in range(4):
                at = lanes(four * 2 + head // 2, head % 2)
                above = part_of((0, 1), slots_at((0, 2), (8, 2)), at)
                below = part_of((2, 3), slots_at((2, 2), (10, 2)), at)
                oa[0 : 2 * BLK, at] += above
                oa[2 * BLK : 4 * BLK, at] += below
            return 0

        lax.fori_loop(0, HEADS // 4, body, 0)

    def attend_region():
        def body(pair, bad):
            one, two = (
                oa[:, lanes(pair, half)] + part_of(range(4), ((REGION_AT, REGION),), lanes(pair, half))
                for half in range(2)
            )
            sums = pltpu.roll(jnp.where(low_half, two, one), HDIM, 1)
            result = jnp.where(low_half, one, two) / sums
            out_ref[:, pl.ds(pl.multiple_of(pair * AUG, AUG), AUG)] = result.astype(jnp.bfloat16)
            fine = (sums >= LOW) & (sums <= HIGH)
            return jnp.maximum(bad, jnp.max(jnp.where(fine, 0.0, 1.0), axis=0, keepdims=True))

        bad = lax.fori_loop(0, HEADS // 2, body, jnp.zeros((1, AUG), jnp.float32))
        flag_ref[0, 0] = jnp.max(bad)

    loads[1].wait()
    keys_values(tokens, 0, OWN)
    q_marks = jnp.concatenate([jnp.broadcast_to(query_marks(b), (BLK, AUG)) for b in range(4)], axis=0)
    project(OWN_KEYS, 0, q_marks.astype(jnp.bfloat16), 0, qa)

    def merge(slots, number):
        total = slots[0].astype(jnp.float32)
        for k in range(1, number):
            total = total + slots[k].astype(jnp.float32)
        return total.astype(jnp.bfloat16)

    attend_own(0, 3)

    halo_wait((0, 1, 2, 3, 4, 5, 6, 7))
    send_halo(both(up, right), halo.at[1], 8, {"col": col + 1})
    send_halo(both(down, left), halo.at[2], 11, {"col": col - 1})
    send_halo(both(right, down), halo.at[7], 9, {"row": row + 1})
    send_halo(both(left, up), halo.at[4], 10, {"row": row - 1})

    arrive1()
    mine[...] = merge(part1, n_row)
    start2()
    part2[col] = mine[...]

    attend_own(3, 6)

    for exists, _, arrives in cnt_copies:
        pl.when(exists)(lambda arrives=arrives: arrives.wait_recv())

    def halo_keys(begin):
        values = halo[begin : begin + 4].reshape(4 * BLK, WIDTH)
        keys_values(values, OWN_KEYS + begin * BLK, SLOTS[begin : begin + 4])

    halo_keys(0)

    arrive2()
    rtok[row] = merge(part2, n_col)
    start3()

    halo_keys(4)

    attend_beside()
    halo_wait((8, 9, 10, 11))
    halo_keys(8)
    attend_across()

    arrive3()
    saves = [
        pltpu.make_async_copy(halo, halo_out, save_sem.at[0]),
        pltpu.make_async_copy(rtok, rtok_out, save_sem.at[1]),
        pltpu.make_async_copy(cnts, cnts_out, save_sem.at[2]),
    ]
    for save in saves:
        save.start()
    keys_values(rtok[...].reshape(REGION, WIDTH), REGION_AT, None)
    attend_region()

    for cond, copy in sends:
        pl.when(cond)(lambda copy=copy: copy.wait_send())
    for exists, copy, _ in cnt_copies:
        pl.when(exists)(lambda copy=copy: copy.wait_send())
    leave1()
    leave2()
    leave3()
    for save in saves:
        save.wait()


def fused(n_row, n_col, tokens, gain, w_qkv, pattern, counts, region):
    chunk = REGION // n_row
    vmem = pl.BlockSpec(memory_space=pltpu.VMEM)
    smem = pl.BlockSpec(memory_space=pltpu.SMEM)
    anywhere = pl.BlockSpec(memory_space=pl.ANY)
    hbm = pl.BlockSpec(memory_space=pltpu.HBM)
    bf16, f32 = jnp.bfloat16, jnp.float32
    dma = pltpu.SemaphoreType.DMA
    flops = 2 * (OWN_KEYS * WIDTH * WIDTH * 3 + (KEYS - OWN_KEYS) * WIDTH * WIDTH * 2 + OWN_KEYS * 1408 * WIDTH * 2)
    return pl.pallas_call(
        functools.partial(kernel, n_row, n_col),
        out_shape=(
            pltpu.VMEM((OWN_KEYS, WIDTH), bf16),
            jax.ShapeDtypeStruct((1, 1), f32),
            jax.ShapeDtypeStruct((len(SLOTS), BLK, WIDTH), bf16),
            jax.ShapeDtypeStruct((n_row, chunk, WIDTH), bf16),
            jax.ShapeDtypeStruct((9, 8, 128), jnp.int32),
        ),
        in_specs=[hbm, hbm, hbm, smem, smem, hbm],
        out_specs=(vmem, smem, anywhere, anywhere, anywhere),
        scratch_shapes=[
            pltpu.VMEM((4, BLK, WIDTH), bf16),
            pltpu.VMEM((len(SLOTS), BLK, WIDTH), bf16),
            pltpu.VMEM((WIDTH, 3 * WIDTH), bf16),
            pltpu.VMEM((9, 8, 128), jnp.int32),
            pltpu.VMEM((n_row, chunk, WIDTH), bf16),
            pltpu.VMEM((n_row, chunk, WIDTH), bf16),
            pltpu.VMEM((chunk, WIDTH), bf16),
            pltpu.VMEM((n_col, chunk, WIDTH), bf16),
            pltpu.VMEM((n_row, chunk, WIDTH), bf16),
            pltpu.VMEM((OWN_KEYS, WIDTH), bf16),
            pltpu.VMEM((OWN_KEYS, HEADS * AUG), bf16),
            pltpu.VMEM((KEYS, HEADS * AUG), bf16),
            pltpu.VMEM((KEYS, HEADS * AUG), bf16),
            pltpu.VMEM((OWN_KEYS, HEADS * AUG), f32),
            pltpu.VMEM((WIDTH,), f32),
            pltpu.VMEM((REGION,), jnp.int32),
            dma((4,)),
            dma((12,)), dma((12,)),
            dma((9,)), dma((9,)),
            dma((n_row,)), dma((n_row,)),
            dma((n_col,)), dma((n_col,)),
            dma((n_row,)), dma((n_row,)),
            dma((3,)),
        ],
        compiler_params=pltpu.CompilerParams(
            collective_id=0, has_side_effects=True, vmem_limit_bytes=48 << 20
        ),
        cost_estimate=pl.CostEstimate(flops=flops, bytes_accessed=9 << 20, transcendentals=OWN_KEYS * 1408 * HEADS),
    )(tokens, gain, w_qkv, pattern, counts, region)


def stable(own, gain, w_qkv, pattern, row, col, n_row, n_col, halo, rtok, cnts):
    grid = {place: own[i] for i, place in enumerate(OWN)}
    grid.update({place: halo[i] for i, place in enumerate(SLOTS)})
    places = [(r, c) for r in range(4) for c in range(4)]
    rows = jnp.concatenate([grid[p] for p in places] + [rtok.reshape(REGION, WIDTH)], axis=0)
    qkv = dot(norm_rows(rows, gain), w_qkv).astype(jnp.bfloat16)
    valid = []
    for place in places:
        (tr, tc), (i, j) = tile_of(place)
        valid.append(jnp.arange(BLK) + (i * 2 + j) * BLK < cnts[3 * tr + tc, 0, 0])
    masks = []
    for block in range(4):
        i, j = divmod(block, 2)
        marks = []
        for number, (r, c) in enumerate(places):
            dr, dc = r - i, c - j
            if 0 <= dr < 3 and 0 <= dc < 3:
                a, b = row * 2 + r - 1, col * 2 + c - 1
                inside = (a >= 0) & (a < 2 * n_row) & (b >= 0) & (b < 2 * n_col)
                marks.append(valid[number] & inside & (pattern[block, 3 * dr + dc] > 0))
            else:
                marks.append(jnp.zeros((BLK,), bool))
        masks.append(jnp.concatenate(marks + [jnp.ones((REGION,), bool)]))
    mask = jnp.stack(masks)
    own_at = jnp.array([4 * r + c for r, c in OWN])
    query = qkv[: 16 * BLK, :WIDTH].reshape(16, BLK, HEADS, HDIM)[own_at]
    key = qkv[:, WIDTH : 2 * WIDTH].reshape(-1, HEADS, HDIM)
    value = qkv[:, 2 * WIDTH :].reshape(-1, HEADS, HDIM)

    def one_head(args):
        q, k, v = args
        scores = jnp.einsum("bqd,kd->bqk", q, k, preferred_element_type=jnp.float32) * (HDIM ** (-0.5))
        masked = jnp.where(mask[:, None, :], scores, -1e30)
        top = jnp.max(masked, axis=-1, keepdims=True)
        weights = jnp.where(mask[:, None, :], jnp.exp(masked - top), 0.0)
        probs = (weights / jnp.sum(weights, axis=-1, keepdims=True)).astype(jnp.bfloat16)
        return jnp.einsum("bqk,kd->bqd", probs, v, preferred_element_type=jnp.float32).astype(jnp.bfloat16)

    heads = lax.map(one_head, (query.transpose(2, 0, 1, 3), key.transpose(1, 0, 2), value.transpose(1, 0, 2)))
    joined = heads.transpose(1, 2, 0, 3).reshape(OWN_KEYS, WIDTH)
    return with_layout_constraint(joined, Layout(major_to_minor=(0, 1)))


def local(n_row, n_col, tokens, gain, w_qkv, pattern, counts, region):
    own = tokens.reshape(4, BLK, WIDTH)
    blocks = pattern.reshape(4, 9)
    out, flag, halo, rtok, cnts = fused(
        n_row, n_col, own, gain, w_qkv, blocks, counts, region
    )
    row, col = lax.axis_index("row"), lax.axis_index("col")
    result = lax.cond(
        flag[0, 0] > 0.0,
        lambda: stable(own, gain.reshape(1, WIDTH), w_qkv, blocks, row, col, n_row, n_col, halo, rtok, cnts),
        lambda: out,
    )
    live = jnp.arange(OWN_KEYS, dtype=jnp.int32) < counts[0, 0]
    return jnp.where(live[:, None], result, jnp.zeros_like(result)).reshape(tokens.shape)


def solution(mesh):
    in_specs = (
        P(("scan", "row"), "col", None, None, None, None),
        P(),
        P(),
        P(("scan", "row"), "col", None, None, None),
        P(("scan", "row"), "col"),
        P("scan"),
    )
    out_specs = P(("scan", "row"), "col", None, None, None, None)
    body = functools.partial(local, mesh.shape["row"], mesh.shape["col"])
    return jax.shard_map(body, mesh=mesh, in_specs=in_specs, out_specs=out_specs, check_vma=False)
```
